32 devices in a mesh: cin: 4 (over x, core), cout: 8 (over z, y).
Axes of the slice: x: 2, y: 2, z: 4, core: 2. Of those that a mesh axis runs over, the one named last changes fastest.
Arguments:
- inputs: bfloat16 [4096, 4, 128], P(('cin', 'cout')), may hold values from -6 to 6
- cotangent: bfloat16 [4096, 4, 128], P(('cout', 'cin')), may hold values from -6 to 6
- matrices: bfloat16 [24, 4096, 4096], P(None, 'cout', 'cin'), may hold values from -0.09375 to 0.09375
- filters: float32 [24, 128], replicated, may hold values from -0.109375 to 0.109375
Outputs:
- matrix_grads: bfloat16 [24, 4096, 4096], P(None, 'cout', 'cin')
- input_grads: bfloat16 [4096, 4, 128], P(('cin', 'cout'))
The draws below stay inside these ranges and needn't reach their ends.
All inputs are finite; a program needn't handle non-finite values.
Results may differ from the reference program's by a relative error of at most 0.002.
Values may be sent and summed in bfloat16 or wider, within the bound.
No kernel may reach another device: no remote copies, remote signals or barrier semaphores. Data moves between devices by JAX's collectives and lax.ppermute only.
A program may use at most 128 MiB of HBM per device.

```python
import jax
import jax.numpy as jnp
from jax import lax

D = 4096
K = 24
B = 4
L = 128


def level_of(stream_key, dims, shards, smallest, high):
    level = 1.0
    for position, parts in shards:
        heights = jax.random.uniform(jax.random.fold_in(jax.random.fold_in(stream_key, 6), position), (parts,), jnp.float32, smallest / len(shards), high / len(shards))
        level = level * jnp.repeat(jnp.exp(heights), dims[position] // parts).reshape((-1,) + (1,) * (len(dims) - 1 - position))
    return level


def normal_values(rng, extent, scale, limit, cuts=(), held_as=jnp.bfloat16):
    entries = scale * jax.random.normal(rng, extent, jnp.float32)
    if cuts:
        entries = entries * level_of(rng, extent, cuts, -0.22, 0.18)
    return jnp.clip(entries, -limit, limit).astype(held_as)


def setup_inputs(seed: int = 0) -> dict:
    keys = jax.random.split(jax.random.key(seed), 5)
    return {
        "inputs": normal_values(keys[0], (D, B, L), 1.0, 6.0, ((0, 32),)),
        "cotangent": normal_values(keys[1], (D, B, L), 1.0, 6.0, ((0, 32),)),
        "matrices": normal_values(keys[2], (K, D, D), D ** -0.5, 0.09375, ((1, 8), (2, 4))),
        "filters": normal_values(keys[3], (K, L), (K * L) ** -0.5, 0.109375, (), jnp.float32),
    }


def toeplitz_upper(filter_row):
    length = filter_row.shape[0]
    padded = jnp.concatenate([filter_row, jnp.zeros((length,), filter_row.dtype)])
    tiled_rows = jnp.tile(padded, length)[: length * (2 * length - 1)]
    return tiled_rows.reshape(length, 2 * length - 1)[:, :length]


def reference(inputs, cotangent, matrices, filters):
    highest = lax.Precision.HIGHEST
    width = inputs.shape[0]
    length = inputs.shape[2]
    inputs_wide = inputs.astype(jnp.float32).reshape(width, -1)
    grads_wide = cotangent.astype(jnp.float32).reshape(width, -1)

    def per_filter(pair):
        filter_row, matrix_tile = pair
        upper_table = toeplitz_upper(filter_row)
        filtered = jnp.dot(inputs_wide.reshape(-1, length), upper_table, precision=highest).reshape(width, -1)
        matrix_grad = jnp.dot(grads_wide, filtered.T, precision=highest).astype(jnp.bfloat16)
        backward = jnp.dot(matrix_tile.astype(jnp.float32).T, grads_wide, precision=highest)
        pulled = jnp.dot(backward.reshape(-1, length), upper_table.T, precision=highest)
        return matrix_grad, pulled.reshape(width, -1)

    matrix_grads, pulled_all = lax.map(per_filter, (filters, matrices))
    total = jnp.sum(pulled_all, axis=0).reshape(inputs.shape)
    return matrix_grads, total.astype(jnp.bfloat16)
```

```python
import functools

import jax
import jax.numpy as jnp
from jax import lax
from jax.experimental import pallas as pl
from jax.experimental.pallas import tpu as pltpu
from jax.sharding import PartitionSpec as P

BF16 = jnp.bfloat16
F32 = jnp.float32
VMEM_LIMIT = 56 * 1024 * 1024


def split(wide):
    high = wide.astype(BF16)
    return high, (wide - high.astype(F32)).astype(BF16)


def dot(left, right):
    return jnp.dot(left, right, preferred_element_type=F32)


def call(body, cost, **kwargs):
    flops, moved = cost
    return pl.pallas_call(
        body,
        compiler_params=pltpu.CompilerParams(vmem_limit_bytes=VMEM_LIMIT),
        cost_estimate=pl.CostEstimate(flops=flops, bytes_accessed=moved, transcendentals=0),
        **kwargs,
    )


def table_kernel(filters_ref, rows_ref, columns_ref):
    count, length = filters_ref.shape
    source = lax.broadcasted_iota(jnp.int32, (length, length), 0)
    token = lax.broadcasted_iota(jnp.int32, (length, length), 1)
    for k in range(count):
        spread = jnp.broadcast_to(filters_ref[k : k + 1, :], (length, length))
        shifted = pltpu.roll(spread, 0, 1, stride=1, stride_axis=0)
        upper = jnp.where(token >= source, shifted, 0.0)
        high, low = split(upper)
        rows_ref[k, :, :length] = high
        rows_ref[k, :, length:] = low
        high, low = split(upper.T)
        columns_ref[:length, k * length : (k + 1) * length] = high
        columns_ref[length:, k * length : (k + 1) * length] = low


def make_tables(filters):
    count, length = filters.shape
    return call(
        table_kernel,
        (count * length * length * 4, count * length * length * 8),
        out_shape=(
            jax.ShapeDtypeStruct((count, length, 2 * length), BF16),
            jax.ShapeDtypeStruct((2 * length, count * length), BF16),
        ),
    )(filters)


def back_kernel(half, per_step, cin_count, pair, *refs):
    pieces = refs[:cin_count]
    place_ref, rows_ref, matrix_ref = refs[cin_count : cin_count + 3]
    outs = refs[cin_count + 3 : -4]
    grads, high, low, total = refs[-4:]
    step = pl.program_id(0)
    length = rows_ref.shape[1]
    seqs = grads.shape[0]
    out_width = grads.shape[2]

    @pl.when(step == 0)
    def _():
        total[...] = jnp.zeros_like(total)
        block = pieces[0].shape[0]
        for r, piece in enumerate(pieces):
            if cin_count == 1:
                columns = slice(None)
            else:
                columns = pl.ds(pl.multiple_of((place_ref[0] ^ r) * block, block), block)
            for b in range(seqs):
                first = (half * seqs + b) * length
                turned = piece[:, first : first + length].astype(F32).T.astype(BF16)
                grads[b, :length, columns] = turned
                grads[b, length:, columns] = turned

    table = rows_ref[...].reshape(per_step * length, 2 * length)
    for b in range(seqs):
        filtered = dot(table, grads[b])
        hi, lo = split(filtered)
        for k in range(per_step):
            rows, columns = slice(b * length, (b + 1) * length), slice(k * out_width, (k + 1) * out_width)
            high[rows, columns] = hi[k * length : (k + 1) * length]
            low[rows, columns] = lo[k * length : (k + 1) * length]
    matrix = matrix_ref[...].reshape(per_step * out_width, -1)
    total[...] += dot(high[...], matrix) + dot(low[...], matrix)

    @pl.when(step == pl.num_programs(0) - 1)
    def _():
        if not pair:
            outs[0][...] = total[...].T
            return
        keep, send = outs
        block = keep.shape[1]
        me = place_ref[1]
        for r in range(keep.shape[0]):
            for out, target in ((keep, me ^ (2 * r)), (send, me ^ (2 * r) ^ 1)):
                columns = pl.ds(pl.multiple_of(target * block, block), block)
                out[r] = total[:, columns].T


def back_half(half, place, pieces, rows, matrices, pair_blocks, per_step=4):
    count, out_width, in_width = matrices.shape
    length = rows.shape[1]
    tokens = pieces[0].shape[1]
    seqs = tokens // length // 2
    width = seqs * length
    if pair_blocks:
        block = in_width // (2 * pair_blocks)
        outs = [jax.ShapeDtypeStruct((pair_blocks, block, width), F32)] * 2
    else:
        outs = [jax.ShapeDtypeStruct((in_width, width), F32)]
    whole = lambda array: pl.BlockSpec(array.shape, lambda i: (0,) * len(array.shape))
    return call(
        functools.partial(back_kernel, half, per_step, len(pieces), bool(pair_blocks)),
        (4 * count * out_width * in_width * width, 2 * matrices.size),
        out_shape=outs,
        grid=(count // per_step,),
        in_specs=[whole(piece) for piece in pieces]
        + [
            pl.BlockSpec(memory_space=pltpu.SMEM),
            pl.BlockSpec((per_step, length, 2 * length), lambda i: (i, 0, 0)),
            pl.BlockSpec((per_step, out_width, in_width), lambda i: (i, 0, 0)),
        ],
        out_specs=[whole(out) for out in outs],
        scratch_shapes=[
            pltpu.VMEM((seqs, 2 * length, out_width), BF16),
            pltpu.VMEM((width, per_step * out_width), BF16),
            pltpu.VMEM((width, per_step * out_width), BF16),
            pltpu.VMEM((width, in_width), F32),
        ],
    )(*pieces, place, rows, matrices)


def matrix_kernel(per_step, cin_count, cout_count, has_base, *refs):
    grad_pieces = refs[:cin_count]
    input_pieces = refs[cin_count : cin_count + cout_count]
    refs = refs[cin_count + cout_count :]
    place_ref, columns_ref = refs[:2]
    out_ref, grads, inputs, parts = refs[2 + has_base :]
    step = pl.program_id(0)
    length = columns_ref.shape[0] // 2
    seqs = grads.shape[0]
    tokens = seqs * length

    @pl.when(step == 0)
    def _():
        block = grad_pieces[0].shape[0]
        for r, piece in enumerate(grad_pieces):
            rows = slice(None)
            if cin_count > 1:
                rows = pl.ds(pl.multiple_of((place_ref[0] ^ r) * block, block), block)
            for b in range(seqs):
                part = piece[:, b * length : (b + 1) * length]
                grads[b, rows, :length] = part
                grads[b, rows, length:] = part
        block = input_pieces[0].shape[0]
        for r, piece in enumerate(input_pieces):
            columns = slice(None)
            if cout_count > 1:
                columns = pl.ds(pl.multiple_of((place_ref[1] ^ r) * block, block), block)
            turned = piece[...].astype(F32).T.astype(BF16)
            inputs[:tokens, columns] = turned
            inputs[tokens:, columns] = turned

    table = columns_ref[...]
    for b in range(seqs):
        hi, lo = split(dot(grads[b], table))
        for k in range(per_step):
            parts[k, :, b * length : (b + 1) * length] = hi[:, k * length : (k + 1) * length]
            parts[k, :, tokens + b * length : tokens + (b + 1) * length] = lo[:, k * length : (k + 1) * length]
    for k in range(per_step):
        out_ref[k] = dot(parts[k], inputs[...]).astype(BF16)


def matrix_range(first, filters, place, grad_pieces, input_pieces, columns, base, shape, per_step=2):
    count, out_width, in_width = shape
    length = columns.shape[0] // 2
    tokens = grad_pieces[0].shape[1]
    seqs = tokens // length
    start = first // per_step
    whole = lambda array: pl.BlockSpec(array.shape, lambda i: (0,) * len(array.shape))
    operands = [*grad_pieces, *input_pieces, place, columns]
    in_specs = [whole(piece) for piece in (*grad_pieces, *input_pieces)] + [
        pl.BlockSpec(memory_space=pltpu.SMEM),
        pl.BlockSpec((2 * length, per_step * length), lambda i: (0, start + i)),
    ]
    aliases = {}
    if base is not None:
        aliases = {len(operands): 0}
        operands.append(base)
        in_specs.append(pl.BlockSpec(memory_space=pl.ANY))
    return call(
        functools.partial(matrix_kernel, per_step, len(grad_pieces), len(input_pieces), base is not None),
        (4 * filters * out_width * in_width * tokens, 2 * filters * out_width * in_width),
        out_shape=jax.ShapeDtypeStruct(shape, BF16),
        grid=(filters // per_step,),
        in_specs=in_specs,
        out_specs=pl.BlockSpec((per_step, out_width, in_width), lambda i: (start + i, 0, 0)),
        scratch_shapes=[
            pltpu.VMEM((seqs, out_width, 2 * length), BF16),
            pltpu.VMEM((2 * tokens, in_width), BF16),
            pltpu.VMEM((per_step, out_width, 2 * tokens), BF16),
        ],
        input_output_aliases=aliases,
    )(*operands)


def add_kernel(keep_ref, came_ref, *outs):
    for r, out in enumerate(outs):
        out[...] = keep_ref[r] + came_ref[r]


def add_pair(keep, came):
    return call(
        add_kernel,
        (keep.size, 12 * keep.size),
        out_shape=[jax.ShapeDtypeStruct(keep.shape[1:], F32)] * keep.shape[0],
    )(keep, came)


def exchange(array, axis, count, flip):
    return lax.ppermute(array, axis, [(i, i ^ flip) for i in range(count)])


def gather_pieces(array, axis, count):
    if count & (count - 1) or array.shape[0] % 128:
        return [lax.all_gather(array, axis, axis=0, tiled=True)]
    return [array] + [exchange(array, axis, count, flip) for flip in range(1, count)]


def shards(cin, cout, inputs, cotangent, matrices, filters):
    own, seq_count, length = inputs.shape
    tokens = seq_count * length
    place = jnp.stack([lax.axis_index("cin"), lax.axis_index("cout")]).astype(jnp.int32)
    grad_pieces = gather_pieces(cotangent.reshape(-1, tokens), "cin", cin)
    input_pieces = gather_pieces(inputs.reshape(-1, tokens), "cout", cout)
    rows, columns = make_tables(filters)
    staged = cout % 2 == 0 and len(input_pieces) == cout
    pair_blocks = cout // 2 if staged else 0
    count = matrices.shape[0]
    middle = count // 2

    first = back_half(0, place, grad_pieces, rows, matrices, pair_blocks)
    second = back_half(1, place, grad_pieces, rows, matrices, pair_blocks)
    if staged:
        came_first = exchange(first[1], "cout", cout, 1)
        came_second = exchange(second[1], "cout", cout, 1)
    build = functools.partial(matrix_range, place=place, grad_pieces=grad_pieces, input_pieces=input_pieces, columns=columns, shape=matrices.shape)
    matrix_grads = build(0, middle, base=None)
    matrix_grads = build(middle, count - middle, base=matrix_grads)
    if staged:
        sums = []
        for keep, came in ((first[0], came_first), (second[0], came_second)):
            mine, *others = add_pair(keep, came)
            for r, other in enumerate(others):
                mine = mine + exchange(other, "cout", cout, 2 * (r + 1))
            sums.append(mine)
    else:
        sums = [lax.psum_scatter(part[0], "cout", scatter_dimension=0, tiled=True) for part in (first, second)]
    summed = jnp.concatenate([part.astype(BF16) for part in sums], axis=1)
    return (matrix_grads, summed.reshape(own, seq_count, length))


def solution(mesh):
    placed = (
        P(("cin", "cout"), None, None),
        P(("cout", "cin"), None, None),
        P(None, "cout", "cin"),
        P(),
    )
    return jax.shard_map(
        functools.partial(shards, mesh.shape["cin"], mesh.shape["cout"]),
        mesh=mesh,
        in_specs=placed,
        out_specs=(P(None, "cout", "cin"), P(("cin", "cout"), None, None)),
        check_vma=False,
    )
```

```python
import functools

import jax
import jax.numpy as jnp
from jax import lax
from jax.experimental import pallas as pl
from jax.experimental.pallas import tpu as pltpu
from jax.sharding import PartitionSpec as P

BF16 = jnp.bfloat16
F32 = jnp.float32
VMEM_LIMIT = 56 * 1024 * 1024


def split(wide):
    high = wide.astype(BF16)
    return high, (wide - high.astype(F32)).astype(BF16)


def dot(left, right):
    return jnp.dot(left, right, preferred_element_type=F32)


def call(body, cost, **kwargs):
    flops, moved = cost
    return pl.pallas_call(
        body,
        compiler_params=pltpu.CompilerParams(vmem_limit_bytes=VMEM_LIMIT),
        cost_estimate=pl.CostEstimate(flops=flops, bytes_accessed=moved, transcendentals=0),
        **kwargs,
    )


def table_kernel(filters_ref, rows_ref):
    count, length = filters_ref.shape
    source = lax.broadcasted_iota(jnp.int32, (length, length), 0)
    token = lax.broadcasted_iota(jnp.int32, (length, length), 1)
    for k in range(count):
        spread = jnp.broadcast_to(filters_ref[k : k + 1, :], (length, length))
        shifted = pltpu.roll(spread, 0, 1, stride=1, stride_axis=0)
        high, low = split(jnp.where(token >= source, shifted, 0.0))
        rows_ref[k, :, :length] = high
        rows_ref[k, :, length:] = low


def make_tables(filters):
    count, length = filters.shape
    return call(
        table_kernel,
        (count * length * length * 4, count * length * length * 4),
        out_shape=jax.ShapeDtypeStruct((count, length, 2 * length), BF16),
    )(filters)


def whole(array):
    return pl.BlockSpec(array.shape, lambda i: (0,) * len(array.shape))


def spot(place, flip, block, count):
    if count == 1:
        return slice(None)
    return pl.ds(pl.multiple_of((place ^ flip) * block, block), block)


def back_kernel(half, cin_count, pair, *refs):
    pieces = refs[:cin_count]
    place_ref, rows_ref, matrix_ref = refs[cin_count : cin_count + 3]
    outs = refs[cin_count + 3 : -4]
    grads, early, late, total = refs[-4:]
    step = pl.program_id(0)
    count, length, _ = rows_ref.shape
    out_width = matrix_ref.shape[1]
    seqs = grads.shape[1] // out_width
    width = seqs * length

    def filter_pair(first, parts):
        table = rows_ref[pl.ds(first, 2)].reshape(2 * length, 2 * length)
        high, low = split(dot(table, grads[...]))
        for b in range(seqs):
            for k in range(2):
                source = slice(k * length, (k + 1) * length), slice(b * out_width, (b + 1) * out_width)
                columns = slice(k * out_width, (k + 1) * out_width)
                parts[b * length : (b + 1) * length, columns] = high[source]
                parts[width + b * length : width + (b + 1) * length, columns] = low[source]

    def add_pair_products(first, parts):
        matrix = matrix_ref[first : first + 2].reshape(2 * out_width, -1)
        total[...] += dot(parts[...], matrix)

    @pl.when(step == 0)
    def _():
        total[...] = jnp.zeros_like(total)
        block = pieces[0].shape[0]
        for b in range(seqs):
            first = (half * seqs + b) * length
            for r, piece in enumerate(pieces):
                turned = piece[:, first : first + length].astype(F32).T.astype(BF16)
                if cin_count == 1:
                    columns = slice(b * out_width, (b + 1) * out_width)
                else:
                    columns = pl.ds(pl.multiple_of(b * out_width + (place_ref[0] ^ r) * block, block), block)
                grads[:length, columns] = turned
                grads[length:, columns] = turned
        filter_pair(0, early)

    filter_pair(4 * step + 2, late)
    add_pair_products(0, early)
    filter_pair(lax.rem(4 * step + 4, count), early)
    add_pair_products(2, late)

    @pl.when(step == pl.num_programs(0) - 1)
    def _():
        if not pair:
            outs[0][...] = (total[:width] + total[width:]).T
            return
        keep, send = outs
        block = keep.shape[1]
        for r in range(keep.shape[0]):
            for out, flip in ((keep, 2 * r), (send, 2 * r + 1)):
                columns = spot(place_ref[1], flip, block, 2)
                out[r] = (total[:width, columns] + total[width:, columns]).T


def back_half(half, place, pieces, rows, matrices, pair_blocks):
    count, out_width, in_width = matrices.shape
    length = rows.shape[1]
    tokens = pieces[0].shape[1]
    seqs = tokens // length // 2
    width = seqs * length
    if pair_blocks:
        block = in_width // (2 * pair_blocks)
        outs = [jax.ShapeDtypeStruct((pair_blocks, block, width), F32)] * 2
    else:
        outs = [jax.ShapeDtypeStruct((in_width, width), F32)]
    return call(
        functools.partial(back_kernel, half, len(pieces), bool(pair_blocks)),
        (4 * count * out_width * in_width * width, 2 * matrices.size),
        out_shape=outs,
        grid=(count // 4,),
        in_specs=[whole(piece) for piece in pieces]
        + [
            pl.BlockSpec(memory_space=pltpu.SMEM),
            whole(rows),
            pl.BlockSpec((4, out_width, in_width), lambda i: (i, 0, 0)),
        ],
        out_specs=[whole(out) for out in outs],
        scratch_shapes=[
            pltpu.VMEM((2 * length, seqs * out_width), BF16),
            pltpu.VMEM((2 * width, 2 * out_width), BF16),
            pltpu.VMEM((2 * width, 2 * out_width), BF16),
            pltpu.VMEM((2 * width, in_width), F32),
        ],
    )(*pieces, place, rows, matrices)


def turn_kernel(cout_count, *refs):
    pieces = refs[:-2]
    place_ref, inputs = refs[-2:]
    tokens = inputs.shape[0] // 2
    block = pieces[0].shape[-2]
    for r, piece in enumerate(pieces):
        for half in range(piece.shape[0]):
            columns = spot(place_ref[1], 2 * half + r, block, cout_count)
            turned = piece[half].astype(F32).T.astype(BF16)
            inputs[:tokens, columns] = turned
            inputs[tokens:, columns] = turned


def turn_inputs(pieces, place, cout_count, in_width):
    tokens = pieces[0].shape[-1]
    in_vmem = pl.BlockSpec(memory_space=pltpu.VMEM)
    return call(
        functools.partial(turn_kernel, cout_count),
        (0, 6 * tokens * in_width),
        in_specs=[in_vmem] * len(pieces) + [pl.BlockSpec(memory_space=pltpu.SMEM)],
        out_specs=in_vmem,
        out_shape=jax.ShapeDtypeStruct((2 * tokens, in_width), BF16),
    )(*pieces, place)


def matrix_kernel(start, cin_count, has_base, *refs):
    pieces = refs[:cin_count]
    place_ref, rows_ref, inputs_ref = refs[cin_count : cin_count + 3]
    out_ref, grads, early, late = refs[cin_count + 3 + has_base :]
    step = pl.program_id(0)
    count, length, _ = rows_ref.shape
    tokens = inputs_ref.shape[0] // 2
    seqs = tokens // length
    out_width = out_ref.shape[1]

    def filter_pair(first, parts):
        table = rows_ref[pl.ds(first, 2)].reshape(2 * length, 2 * length)
        filtered = lax.dot_general(grads[...], table, (((1,), (1,)), ((), ())), preferred_element_type=F32)
        high, low = split(filtered)
        for b in range(seqs):
            for k in range(2):
                source = slice(b * out_width, (b + 1) * out_width), slice(k * length, (k + 1) * length)
                rows = slice(k * out_width, (k + 1) * out_width)
                parts[rows, b * length : (b + 1) * length] = high[source]
                parts[rows, tokens + b * length : tokens + (b + 1) * length] = low[source]

    def write_pair(first, parts):
        product = dot(parts[...], inputs_ref[...]).astype(BF16)
        out_ref[first : first + 2] = product.reshape(2, out_width, -1)

    @pl.when(step == 0)
    def _():
        block = pieces[0].shape[0]
        for b in range(seqs):
            for r, piece in enumerate(pieces):
                if cin_count == 1:
                    rows = slice(b * out_width, (b + 1) * out_width)
                else:
                    rows = pl.ds(pl.multiple_of(b * out_width + (place_ref[0] ^ r) * block, block), block)
                part = piece[:, b * length : (b + 1) * length]
                grads[rows, :length] = part
                grads[rows, length:] = part
        filter_pair(start, early)

    filter_pair(start + 4 * step + 2, late)
    write_pair(0, early)
    filter_pair(lax.rem(start + 4 * step + 4, count), early)
    write_pair(2, late)


def matrix_range(start, filters, base, place, pieces, inputs, rows, shape):
    _, out_width, in_width = shape
    length = rows.shape[1]
    tokens = inputs.shape[0] // 2
    seqs = tokens // length
    operands = [*pieces, place, rows, inputs]
    in_specs = [whole(piece) for piece in pieces] + [pl.BlockSpec(memory_space=pltpu.SMEM), whole(rows), whole(inputs)]
    aliases = {}
    if base is not None:
        aliases = {len(operands): 0}
        operands.append(base)
        in_specs.append(pl.BlockSpec(memory_space=pl.ANY))
    return call(
        functools.partial(matrix_kernel, start, len(pieces), base is not None),
        (4 * filters * out_width * in_width * tokens, 2 * filters * out_width * in_width),
        out_shape=jax.ShapeDtypeStruct(shape, BF16),
        grid=(filters // 4,),
        in_specs=in_specs,
        out_specs=pl.BlockSpec((4, out_width, in_width), lambda i: (start // 4 + i, 0, 0)),
        scratch_shapes=[
            pltpu.VMEM((seqs * out_width, 2 * length), BF16),
            pltpu.VMEM((2 * out_width, 2 * tokens), BF16),
            pltpu.VMEM((2 * out_width, 2 * tokens), BF16),
        ],
        input_output_aliases=aliases,
    )(*operands)


def add_kernel(keep_ref, came_ref, *outs):
    for r, out in enumerate(outs):
        out[...] = keep_ref[r] + came_ref[r]


def add_pair(keep, came):
    return call(
        add_kernel,
        (keep.size, 12 * keep.size),
        out_shape=[jax.ShapeDtypeStruct(keep.shape[1:], F32)] * keep.shape[0],
    )(keep, came)


def exchange(array, axis, count, flip):
    return lax.ppermute(array, axis, [(i, i ^ flip) for i in range(count)])


def after(array, *others):
    return lax.optimization_barrier((array, *others))[0]


def shards(cin, cout, inputs, cotangent, matrices, filters):
    own, seq_count, length = inputs.shape
    tokens = seq_count * length
    count, out_width, in_width = matrices.shape
    place = jnp.stack([lax.axis_index("cin"), lax.axis_index("cout")]).astype(jnp.int32)
    flat_grads = cotangent.reshape(-1, tokens)
    flat_inputs = inputs.reshape(-1, tokens)
    if cin & (cin - 1) or flat_grads.shape[0] % 128:
        pieces = [lax.all_gather(flat_grads, "cin", axis=0, tiled=True)]
    else:
        pieces = [flat_grads] + [exchange(flat_grads, "cin", cin, flip) for flip in range(1, cin)]
    rows = make_tables(filters)
    staged = cout & (cout - 1) == 0 and cout > 1 and own % 128 == 0
    pair_blocks = cout // 2 if staged else 0
    if staged:
        columns = [flat_inputs] + [exchange(flat_inputs, "cout", cout, 2 * r) for r in range(1, pair_blocks)]

    first = back_half(0, place, pieces, rows, matrices, pair_blocks)
    if staged:
        came_first = exchange(first[1], "cout", cout, 1)
        mine = jnp.stack(after(columns, first[0]))
        input_pieces = [mine, exchange(mine, "cout", cout, 1)]
    else:
        input_pieces = [lax.all_gather(flat_inputs, "cout", axis=0, tiled=True)[None]]
    second = back_half(1, after(place, first[0]), pieces, rows, matrices, pair_blocks)
    if staged:
        came_second = exchange(second[1], "cout", cout, 1)
    turned = turn_inputs(input_pieces, after(place, second[0]), cout if staged else 1, in_width)

    build = functools.partial(matrix_range, pieces=pieces, inputs=turned, rows=rows, shape=matrices.shape)
    sixth = count // 6
    grads = build(0, sixth, None, place)
    if staged:
        sums = []
        halves = ((sixth, 3 * sixth, first[0], came_first), (3 * sixth, count, second[0], came_second))
        for start, stop, keep, came in halves:
            keep = after(keep, grads)
            mine, *others = add_pair(keep, came)
            place = after(place, mine)
            sums.append([mine] + [exchange(other, "cout", cout, 2 * (r + 1)) for r, other in enumerate(others)])
            grads = build(start, stop - start, grads, place)
        sums = [functools.reduce(jnp.add, terms) for terms in sums]
    else:
        grads = build(sixth, count - sixth, grads, place)
        sums = [lax.psum_scatter(part[0], "cout", scatter_dimension=0, tiled=True) for part in (first, second)]
    summed = jnp.concatenate(sums, axis=1).astype(BF16)
    return (grads, summed.reshape(own, seq_count, length))


def solution(mesh):
    placed = (
        P(("cin", "cout"), None, None),
        P(("cout", "cin"), None, None),
        P(None, "cout", "cin"),
        P(),
    )
    return jax.shard_map(
        functools.partial(shards, mesh.shape["cin"], mesh.shape["cout"]),
        mesh=mesh,
        in_specs=placed,
        out_specs=(P(None, "cout", "cin"), P(("cin", "cout"), None, None)),
        check_vma=False,
    )
```

```python
import functools

import jax
import jax.numpy as jnp
from jax import lax
from jax.experimental import pallas as pl
from jax.experimental.pallas import tpu as pltpu
from jax.sharding import PartitionSpec as P

BF16 = jnp.bfloat16
F16 = jnp.float16
F32 = jnp.float32
F8 = jnp.float8_e4m3fn
MIB = 1024 * 1024
TINY = 1e-30


def split(wide):
    high = wide.astype(BF16)
    return high, wide - high.astype(F32)


def dot(left, right):
    return jnp.dot(left, right, preferred_element_type=F32)


def call(body, cost, limit, **kwargs):
    flops, moved = cost
    return pl.pallas_call(
        body,
        compiler_params=pltpu.CompilerParams(vmem_limit_bytes=limit * MIB),
        cost_estimate=pl.CostEstimate(flops=flops, bytes_accessed=moved, transcendentals=0),
        **kwargs,
    )


def whole(array):
    return pl.BlockSpec(array.shape, lambda i: (0,) * len(array.shape))


def largest(array):
    return jnp.max(jnp.abs(array.astype(F32)), keepdims=True)


def spot(axis, flip, block, count, base=0):
    if count == 1:
        return slice(base, base + block)
    return pl.ds(pl.multiple_of(base + (lax.axis_index(axis) ^ flip) * block, block), block)


def table_kernel(filters_ref, rows_ref):
    count, length = filters_ref.shape
    source = lax.broadcasted_iota(jnp.int32, (length, length), 0)
    token = lax.broadcasted_iota(jnp.int32, (length, length), 1)
    for k in range(count):
        spread = jnp.broadcast_to(filters_ref[k : k + 1, :], (length, length))
        shifted = pltpu.roll(spread, 0, 1, stride=1, stride_axis=0)
        high, low = split(jnp.where(token >= source, shifted, 0.0))
        rows_ref[k, :, :length] = high
        rows_ref[k, :, length:] = low.astype(BF16)


def make_tables(filters):
    count, length = filters.shape
    return call(
        table_kernel,
        (count * length * length * 4, count * length * length * 4),
        8,
        out_shape=jax.ShapeDtypeStruct((count, length, 2 * length), BF16),
    )(filters)


def back_kernel(cin_count, *refs):
    pieces = refs[:cin_count]
    rows_ref, matrix_ref, out, grads, parts, total = refs[cin_count:]
    step = pl.program_id(0)
    _, length, _ = rows_ref.shape
    out_width = matrix_ref.shape[1]
    seqs = grads.shape[1] // out_width
    tokens = seqs * length

    @pl.when(step == 0)
    def _():
        total[...] = jnp.zeros_like(total)
        block = pieces[0].shape[0]
        for b in range(seqs):
            for r, piece in enumerate(pieces):
                turned = piece[:, b * length : (b + 1) * length].astype(F32).T.astype(BF16)
                columns = spot("cin", r, block, cin_count, b * out_width)
                grads[:length, columns] = turned
                grads[length:, columns] = turned

    table = rows_ref[pl.ds(2 * step, 2)].reshape(2 * length, 2 * length)
    for b in range(seqs):
        high, low = split(dot(table, grads[:, b * out_width : (b + 1) * out_width]))
        low = low.astype(BF16)
        for k in range(2):
            source, columns = slice(k * length, (k + 1) * length), slice(k * out_width, (k + 1) * out_width)
            parts[b * length : (b + 1) * length, columns] = high[source]
            parts[tokens + b * length : tokens + (b + 1) * length, columns] = low[source]
    matrix = matrix_ref[...].reshape(2 * out_width, -1)
    total[...] += dot(parts[:tokens], matrix) + dot(parts[tokens:], matrix)

    @pl.when(step == pl.num_programs(0) - 1)
    def _():
        summed = total[...]
        exponent = jnp.floor(jnp.log2(jnp.maximum(largest(summed), TINY))) + 1.0
        summed = summed * jnp.exp2(14.0 - exponent)
        block = out.shape[1] - 8
        turned = [] if block % 128 == 0 else [summed.T]
        for j in range(out.shape[0]):
            place = slice(j * block, (j + 1) * block)
            out[j, :block] = turned[0][place] if turned else summed[:, place].T
            out[j, block:] = jnp.broadcast_to(exponent, (8, tokens))


def back_sums(pieces, rows, matrices, cout):
    count, out_width, in_width = matrices.shape
    length = rows.shape[1]
    tokens = pieces[0].shape[1]
    seqs = tokens // length
    out = jax.ShapeDtypeStruct((cout, in_width // cout + 8, tokens), F32)
    return call(
        functools.partial(back_kernel, len(pieces)),
        (4 * count * out_width * in_width * tokens, 2 * matrices.size),
        32,
        out_shape=out,
        grid=(count // 2,),
        in_specs=[whole(piece) for piece in pieces]
        + [whole(rows), pl.BlockSpec((2, out_width, in_width), lambda i: (i, 0, 0))],
        out_specs=whole(out),
        scratch_shapes=[
            pltpu.VMEM((2 * length, seqs * out_width), BF16),
            pltpu.VMEM((2 * tokens, 2 * out_width), BF16),
            pltpu.VMEM((tokens, in_width), F32),
        ],
    )(*pieces, rows, matrices)


def matrix_kernel(cin_count, input_count, cout_count, *refs):
    pieces = refs[:cin_count]
    input_pieces = refs[cin_count : cin_count + input_count]
    rows_ref, out_ref, grads, inputs, inputs8, parts, parts8, bounds = refs[cin_count + input_count :]
    step = pl.program_id(0)
    _, length, _ = rows_ref.shape
    tokens = inputs.shape[0]
    seqs = tokens // length
    out_width = out_ref.shape[1]

    @pl.when(step == 0)
    def _():
        block = pieces[0].shape[0]
        for r, piece in enumerate(pieces):
            for b in range(seqs):
                rows = spot("cin", r, block, cin_count, b * out_width)
                part = piece[:, b * length : (b + 1) * length]
                grads[rows, :length] = part
                grads[rows, length:] = part
        gmax = functools.reduce(jnp.maximum, [largest(piece[...]) for piece in pieces])
        xmax = functools.reduce(jnp.maximum, [largest(piece[half]) for piece in input_pieces for half in range(piece.shape[0])])
        xmax = jnp.maximum(xmax, TINY)
        bounds[0:1, :] = jnp.broadcast_to(gmax, (1, length))
        bounds[1:2, :] = jnp.broadcast_to(xmax, (1, length))
        block = input_pieces[0].shape[1]
        for r, piece in enumerate(input_pieces):
            for half in range(piece.shape[0]):
                columns = spot("cout", 2 * r + half, block, cout_count)
                turned = piece[half].astype(F32).T
                inputs[:, columns] = turned.astype(BF16)
                inputs8[:, columns] = (turned * (256.0 / xmax)).astype(F8)

    table = rows_ref[pl.ds(2 * step, 2)]
    reach = [
        jnp.maximum(jnp.sum(jnp.abs(table[k, 0:1, :length].astype(F32)), keepdims=True) * bounds[0:1, 0:1], TINY)
        for k in range(2)
    ]
    table = table.reshape(2 * length, 2 * length)
    for b in range(seqs):
        place = slice(b * length, (b + 1) * length)
        filtered = lax.dot_general(
            grads[b * out_width : (b + 1) * out_width], table, (((1,), (1,)), ((), ())), preferred_element_type=F32
        )
        high, low = split(filtered)
        for k in range(2):
            source = slice(k * length, (k + 1) * length)
            rows = slice(k * out_width, (k + 1) * out_width)
            parts[rows, place] = high[:, source]
            parts8[rows, place] = (low[:, source] * (65536.0 / reach[k])).astype(F8)
    for k in range(2):
        rows = slice(k * out_width, (k + 1) * out_width)
        back = (reach[k] / 65536.0) * (bounds[1:2, 0:1] / 256.0)
        product = dot(parts[rows], inputs[...]) + dot(parts8[rows], inputs8[...]) * back
        out_ref[k] = product.astype(BF16)


def matrix_sums(pieces, input_pieces, rows, cout_count, shape):
    count, out_width, in_width = shape
    length = rows.shape[1]
    tokens = pieces[0].shape[1]
    seqs = tokens // length
    return call(
        functools.partial(matrix_kernel, len(pieces), len(input_pieces), cout_count),
        (3 * count * out_width * in_width * tokens, 2 * count * out_width * in_width),
        32,
        out_shape=jax.ShapeDtypeStruct(shape, BF16),
        grid=(count // 2,),
        in_specs=[whole(piece) for piece in (*pieces, *input_pieces)] + [whole(rows)],
        out_specs=pl.BlockSpec((2, out_width, in_width), lambda i: (i, 0, 0)),
        scratch_shapes=[
            pltpu.VMEM((seqs * out_width, 2 * length), BF16),
            pltpu.VMEM((tokens, in_width), BF16),
            pltpu.VMEM((tokens, in_width), F8),
            pltpu.VMEM((2 * out_width, tokens), BF16),
            pltpu.VMEM((2 * out_width, tokens), F8),
            pltpu.VMEM((8, length), F32),
        ],
    )(*pieces, *input_pieces, rows)


def exchange(array, axis, count, flip):
    return lax.ppermute(array, axis, [(i, i ^ flip) for i in range(count)])


def shards(cin, cout, inputs, cotangent, matrices, filters):
    own, seq_count, length = inputs.shape
    tokens = seq_count * length
    flat_grads = cotangent.reshape(-1, tokens)
    if cin & (cin - 1) or flat_grads.shape[0] % 128:
        pieces = [lax.all_gather(flat_grads, "cin", axis=0, tiled=True)]
    else:
        pieces = [flat_grads] + [exchange(flat_grads, "cin", cin, flip) for flip in range(1, cin)]
    rows = make_tables(filters)
    flat_inputs = inputs.reshape(-1, tokens)
    if cout < 2 or cout & (cout - 1) or own % 128:
        input_pieces = [lax.all_gather(flat_inputs, "cout", axis=0, tiled=True)[None]]
        cout_count = 1
    else:
        both = jnp.stack([flat_inputs, exchange(flat_inputs, "cout", cout, 1)])
        input_pieces = [both] + [exchange(both, "cout", cout, flip) for flip in range(2, cout, 2)]
        cout_count = cout

    blocks = back_sums(pieces, rows, matrices, cout).astype(F16)
    came = lax.all_to_all(blocks, "cout", 0, 0, tiled=True).astype(F32)
    matrix_grads = matrix_sums(pieces, input_pieces, rows, cout_count, matrices.shape)
    scales = jnp.exp2(came[:, own : own + 1] - 14.0)
    input_grads = jnp.sum(came[:, :own] * scales, axis=0).astype(BF16)
    return (matrix_grads, input_grads.reshape(own, seq_count, length))


def solution(mesh):
    placed = (
        P(("cin", "cout"), None, None),
        P(("cout", "cin"), None, None),
        P(None, "cout", "cin"),
        P(),
    )
    return jax.shard_map(
        functools.partial(shards, mesh.shape["cin"], mesh.shape["cout"]),
        mesh=mesh,
        in_specs=placed,
        out_specs=(P(None, "cout", "cin"), P(("cin", "cout"), None, None)),
        check_vma=False,
    )
```

```python
import functools

import jax
import jax.numpy as jnp
from jax import lax
from jax.experimental import pallas as pl
from jax.experimental.pallas import tpu as pltpu
from jax.sharding import PartitionSpec as P

BF16 = jnp.bfloat16
F16 = jnp.float16
F32 = jnp.float32
F8 = jnp.float8_e4m3fn
MIB = 1024 * 1024
TINY = 1e-30


def split(wide):
    high = wide.astype(BF16)
    return high, wide - high.astype(F32)


def dot(left, right):
    return jnp.dot(left, right, preferred_element_type=F32)


def call(body, cost, limit, **kwargs):
    flops, moved = cost
    return pl.pallas_call(
        body,
        compiler_params=pltpu.CompilerParams(vmem_limit_bytes=limit * MIB),
        cost_estimate=pl.CostEstimate(flops=flops, bytes_accessed=moved, transcendentals=0),
        **kwargs,
    )


def whole(array):
    return pl.BlockSpec(array.shape, lambda i: (0,) * len(array.shape))


def largest(array):
    return jnp.max(jnp.abs(array.astype(F32)), keepdims=True)


def spot(axis, flip, block, count, base=0):
    if count == 1:
        return slice(base, base + block)
    return pl.ds(pl.multiple_of(base + (lax.axis_index(axis) ^ flip) * block, block), block)


def reach_of(table, gmax):
    length = table.shape[1]
    sums = [jnp.sum(jnp.abs(table[k, 0:1, :length].astype(F32)), keepdims=True) for k in range(2)]
    return [jnp.maximum(total * gmax, TINY) for total in sums]


def table_kernel(filters_ref, rows_ref):
    count, length = filters_ref.shape
    source = lax.broadcasted_iota(jnp.int32, (length, length), 0)
    token = lax.broadcasted_iota(jnp.int32, (length, length), 1)
    for k in range(count):
        spread = jnp.broadcast_to(filters_ref[k : k + 1, :], (length, length))
        shifted = pltpu.roll(spread, 0, 1, stride=1, stride_axis=0)
        high, low = split(jnp.where(token >= source, shifted, 0.0))
        rows_ref[k, :, :length] = high
        rows_ref[k, :, length:] = low.astype(BF16)


def make_tables(filters):
    count, length = filters.shape
    return call(
        table_kernel,
        (count * length * length * 4, count * length * length * 4),
        8,
        out_shape=jax.ShapeDtypeStruct((count, length, 2 * length), BF16),
    )(filters)


def back_kernel(cin_count, *refs):
    pieces = refs[:cin_count]
    rows_ref, matrix_ref, out, grads, parts, parts8, total, bounds = refs[cin_count:]
    step = pl.program_id(0)
    _, length, _ = rows_ref.shape
    out_width = matrix_ref.shape[1]
    seqs = grads.shape[1] // out_width
    tokens = seqs * length

    @pl.when(step == 0)
    def _():
        total[...] = jnp.zeros_like(total)
        block = pieces[0].shape[0]
        for b in range(seqs):
            for r, piece in enumerate(pieces):
                turned = piece[:, b * length : (b + 1) * length].astype(F32).T.astype(BF16)
                columns = spot("cin", r, block, cin_count, b * out_width)
                grads[:length, columns] = turned
                grads[length:, columns] = turned
        gmax = functools.reduce(jnp.maximum, [largest(piece[...]) for piece in pieces])
        bounds[...] = jnp.broadcast_to(gmax, bounds.shape)

    matrix = matrix_ref[...].reshape(2 * out_width, -1)
    peak = jnp.max(jnp.abs(matrix).reshape(-1, 16, matrix.shape[1]), axis=0)
    matrix_scale = (256.0 / jnp.maximum(largest(peak), TINY)).astype(BF16)
    matrix8 = (matrix * matrix_scale).astype(F8)
    table = rows_ref[pl.ds(2 * step, 2)]
    reach = reach_of(table, bounds[0:1, 0:1])
    reach = jnp.maximum(reach[0], reach[1])
    table = table.reshape(2 * length, 2 * length)
    for b in range(seqs):
        high, low = split(dot(table, grads[:, b * out_width : (b + 1) * out_width]))
        low = (low * (65536.0 / reach)).astype(F8)
        for k in range(2):
            source, columns = slice(k * length, (k + 1) * length), slice(k * out_width, (k + 1) * out_width)
            parts[b * length : (b + 1) * length, columns] = high[source]
            parts8[b * length : (b + 1) * length, columns] = low[source]
    back = (reach / 65536.0) / matrix_scale.astype(F32)
    total[...] += dot(parts[...], matrix) + dot(parts8[...], matrix8) * back

    @pl.when(step == pl.num_programs(0) - 1)
    def _():
        summed = total[...]
        exponent = jnp.floor(jnp.log2(jnp.maximum(largest(summed), TINY))) + 1.0
        summed = summed * jnp.exp2(14.0 - exponent)
        block = out.shape[1] - 8
        turned = [] if block % 128 == 0 else [summed.T]
        for j in range(out.shape[0]):
            place = slice(j * block, (j + 1) * block)
            out[j, :block] = turned[0][place] if turned else summed[:, place].T
            out[j, block:] = jnp.broadcast_to(exponent, (8, tokens))


def back_sums(pieces, rows, matrices, cout):
    count, out_width, in_width = matrices.shape
    length = rows.shape[1]
    tokens = pieces[0].shape[1]
    seqs = tokens // length
    out = jax.ShapeDtypeStruct((cout, in_width // cout + 8, tokens), F32)
    return call(
        functools.partial(back_kernel, len(pieces)),
        (4 * count * out_width * in_width * tokens, 2 * matrices.size),
        32,
        out_shape=out,
        grid=(count // 2,),
        in_specs=[whole(piece) for piece in pieces]
        + [whole(rows), pl.BlockSpec((2, out_width, in_width), lambda i: (i, 0, 0))],
        out_specs=whole(out),
        scratch_shapes=[
            pltpu.VMEM((2 * length, seqs * out_width), BF16),
            pltpu.VMEM((tokens, 2 * out_width), BF16),
            pltpu.VMEM((tokens, 2 * out_width), F8),
            pltpu.VMEM((tokens, in_width), F32),
            pltpu.VMEM((8, length), F32),
        ],
    )(*pieces, rows, matrices)


def matrix_kernel(cin_count, input_count, cout_count, *refs):
    pieces = refs[:cin_count]
    input_pieces = refs[cin_count : cin_count + input_count]
    rows_ref, out_ref, grads, inputs, inputs8, parts, parts8, bounds = refs[cin_count + input_count :]
    step = pl.program_id(0)
    _, length, _ = rows_ref.shape
    tokens = inputs.shape[0]
    seqs = tokens // length
    out_width = out_ref.shape[1]

    @pl.when(step == 0)
    def _():
        block = pieces[0].shape[0]
        for r, piece in enumerate(pieces):
            for b in range(seqs):
                rows = spot("cin", r, block, cin_count, b * out_width)
                part = piece[:, b * length : (b + 1) * length]
                grads[rows, :length] = part
                grads[rows, length:] = part
        gmax = functools.reduce(jnp.maximum, [largest(piece[...]) for piece in pieces])
        xmax = functools.reduce(jnp.maximum, [largest(piece[half]) for piece in input_pieces for half in range(piece.shape[0])])
        xmax = jnp.maximum(xmax, TINY)
        bounds[0:1, :] = jnp.broadcast_to(gmax, (1, length))
        bounds[1:2, :] = jnp.broadcast_to(xmax, (1, length))
        block = input_pieces[0].shape[1]
        for r, piece in enumerate(input_pieces):
            for half in range(piece.shape[0]):
                columns = spot("cout", 2 * r + half, block, cout_count)
                turned = piece[half].astype(F32).T
                inputs[:, columns] = turned.astype(BF16)
                inputs8[:, columns] = (turned * (256.0 / xmax)).astype(F8)

    def pair(p, _):
        table = rows_ref[pl.ds(4 * step + 2 * p, 2)]
        reach = reach_of(table, bounds[0:1, 0:1])
        table = table.reshape(2 * length, 2 * length)
        for k in range(2):
            back = (reach[k] / 65536.0) * (bounds[1:2, 0:1] / 256.0)
            bounds[2 + k : 3 + k, :] = jnp.broadcast_to(back, (1, length))

        def sequence(b, _):
            place = pl.ds(pl.multiple_of(b * length, length), length)
            source = grads[pl.ds(pl.multiple_of(b * out_width, out_width), out_width)]
            filtered = lax.dot_general(source, table, (((1,), (1,)), ((), ())), preferred_element_type=F32)
            high, low = split(filtered)
            for k in range(2):
                columns = slice(k * length, (k + 1) * length)
                parts[k, :, place] = high[:, columns]
                parts8[k, :, place] = (low[:, columns] * (65536.0 / reach[k])).astype(F8)
            return _

        lax.fori_loop(0, seqs, sequence, 0)

        def product(k, _):
            back = bounds[pl.ds(2 + k, 1), 0:1]
            total = dot(parts[k], inputs[...]) + dot(parts8[k], inputs8[...]) * back
            out_ref[2 * p + k] = total.astype(BF16)
            return _

        return lax.fori_loop(0, 2, product, 0)

    lax.fori_loop(0, 2, pair, 0)


def matrix_sums(pieces, input_pieces, rows, cout_count, shape):
    count, out_width, in_width = shape
    length = rows.shape[1]
    tokens = pieces[0].shape[1]
    seqs = tokens // length
    return call(
        functools.partial(matrix_kernel, len(pieces), len(input_pieces), cout_count),
        (3 * count * out_width * in_width * tokens, 2 * count * out_width * in_width),
        32,
        out_shape=jax.ShapeDtypeStruct(shape, BF16),
        grid=(count // 4,),
        in_specs=[whole(piece) for piece in (*pieces, *input_pieces)] + [whole(rows)],
        out_specs=pl.BlockSpec((4, out_width, in_width), lambda i: (i, 0, 0)),
        scratch_shapes=[
            pltpu.VMEM((seqs * out_width, 2 * length), BF16),
            pltpu.VMEM((tokens, in_width), BF16),
            pltpu.VMEM((tokens, in_width), F8),
            pltpu.VMEM((2, out_width, tokens), BF16),
            pltpu.VMEM((2, out_width, tokens), F8),
            pltpu.VMEM((8, length), F32),
        ],
    )(*pieces, *input_pieces, rows)


def exchange(array, axis, count, flip):
    return lax.ppermute(array, axis, [(i, i ^ flip) for i in range(count)])


def shards(cin, cout, inputs, cotangent, matrices, filters):
    own, seq_count, length = inputs.shape
    tokens = seq_count * length
    flat_grads = cotangent.reshape(-1, tokens)
    if cin & (cin - 1) or flat_grads.shape[0] % 128:
        pieces = [lax.all_gather(flat_grads, "cin", axis=0, tiled=True)]
    else:
        pieces = [flat_grads] + [exchange(flat_grads, "cin", cin, flip) for flip in range(1, cin)]
    rows = make_tables(lax.optimization_barrier((filters, flat_grads))[0])
    flat_inputs = inputs.reshape(-1, tokens)
    if cout < 2 or cout & (cout - 1) or own % 128:
        input_pieces = [lax.all_gather(flat_inputs, "cout", axis=0, tiled=True)[None]]
        cout_count = 1
    else:
        both = jnp.concatenate([flat_inputs, exchange(flat_inputs, "cout", cout, 1)]).reshape(2, own, tokens)
        input_pieces = [both] + [exchange(both, "cout", cout, flip) for flip in range(2, cout, 2)]
        cout_count = cout

    blocks = back_sums(pieces, rows, matrices, cout).astype(F16)
    came = lax.all_to_all(blocks, "cout", 0, 0, tiled=True)
    matrix_grads = matrix_sums(pieces, input_pieces, rows, cout_count, matrices.shape)
    scales = jnp.exp2(came[:, own : own + 1].astype(F32) - 14.0)
    input_grads = jnp.sum(came[:, :own].astype(F32) * scales, axis=0).astype(BF16)
    return (matrix_grads, input_grads.reshape(own, seq_count, length))


def solution(mesh):
    placed = (
        P(("cin", "cout"), None, None),
        P(("cout", "cin"), None, None),
        P(None, "cout", "cin"),
        P(),
    )
    return jax.shard_map(
        functools.partial(shards, mesh.shape["cin"], mesh.shape["cout"]),
        mesh=mesh,
        in_specs=placed,
        out_specs=(P(None, "cout", "cin"), P(("cin", "cout"), None, None)),
        check_vma=False,
    )
```

```python
import functools

import jax
import jax.numpy as jnp
from jax import lax
from jax.experimental import pallas as pl
from jax.experimental.pallas import tpu as pltpu
from jax.sharding import PartitionSpec as P

BF16 = jnp.bfloat16
F16 = jnp.float16
F32 = jnp.float32
F8 = jnp.float8_e4m3fn
MIB = 1024 * 1024
TINY = 1e-18
RANGE = 2.0**24


def split(wide):
    high = wide.astype(BF16)
    return high, wide - high.astype(F32)


def dot(left, right):
    return jnp.dot(left, right, preferred_element_type=F32)


def call(body, cost, limit, **kwargs):
    flops, moved = cost
    return pl.pallas_call(
        body,
        compiler_params=pltpu.CompilerParams(vmem_limit_bytes=limit * MIB),
        cost_estimate=pl.CostEstimate(flops=flops, bytes_accessed=moved, transcendentals=0),
        **kwargs,
    )


def whole(array):
    return pl.BlockSpec(array.shape, lambda i: (0,) * len(array.shape))


def largest(array):
    return jnp.max(jnp.abs(array.astype(F32)), keepdims=True)


def spot(axis, flip, block, count, base=0):
    if count == 1:
        return slice(base, base + block)
    return pl.ds(pl.multiple_of(base + (lax.axis_index(axis) ^ flip) * block, block), block)


def reach_of(table, gmax):
    length = table.shape[1]
    sums = [jnp.sum(jnp.abs(table[k, 0:1, :length].astype(F32)), keepdims=True) for k in range(2)]
    return [jnp.maximum(total, TINY) * jnp.maximum(gmax, TINY) for total in sums]


def table_kernel(filters_ref, rows_ref, columns_ref):
    count, length = filters_ref.shape
    source = lax.broadcasted_iota(jnp.int32, (length, length), 0)
    token = lax.broadcasted_iota(jnp.int32, (length, length), 1)
    for k in range(count):
        spread = jnp.broadcast_to(filters_ref[k : k + 1, :], (length, length))
        shifted = pltpu.roll(spread, 0, 1, stride=1, stride_axis=0)
        upper = jnp.where(token >= source, shifted, 0.0)
        high, low = split(upper)
        rows_ref[k, :, :length] = high
        rows_ref[k, :, length:] = low.astype(BF16)
        high, low = split(upper.T)
        columns_ref[k // 2, :length, k % 2 * length : (k % 2 + 1) * length] = high
        columns_ref[k // 2, length:, k % 2 * length : (k % 2 + 1) * length] = low.astype(BF16)


def make_tables(filters):
    count, length = filters.shape
    return call(
        table_kernel,
        (count * length * length * 4, count * length * length * 8),
        16,
        out_shape=(
            jax.ShapeDtypeStruct((count, length, 2 * length), BF16),
            jax.ShapeDtypeStruct((count // 2, 2 * length, 2 * length), BF16),
        ),
    )(filters)


def back_kernel(cin_count, *refs):
    pieces = refs[:cin_count]
    rows_ref, matrix_ref, out, grads, parts, parts8, total, bounds = refs[cin_count:]
    step = pl.program_id(0)
    _, length, _ = rows_ref.shape
    out_width = matrix_ref.shape[1]
    seqs = grads.shape[1] // out_width
    tokens = seqs * length

    @pl.when(step == 0)
    def _():
        total[...] = jnp.zeros_like(total)
        block = pieces[0].shape[0]
        for b in range(seqs):
            for r, piece in enumerate(pieces):
                turned = piece[:, b * length : (b + 1) * length].astype(F32).T.astype(BF16)
                columns = spot("cin", r, block, cin_count, b * out_width)
                grads[:length, columns] = turned
                grads[length:, columns] = turned
        gmax = functools.reduce(jnp.maximum, [largest(piece[...]) for piece in pieces])
        bounds[...] = jnp.broadcast_to(gmax, bounds.shape)

    matrix = matrix_ref[...].reshape(2 * out_width, -1)
    peak = jnp.max(jnp.abs(matrix).reshape(-1, 16, matrix.shape[1]), axis=0)
    peak = jnp.maximum(largest(peak), TINY)
    matrix_scale = (256.0 / peak).astype(BF16)
    matrix8 = (matrix * matrix_scale).astype(F8)
    table = rows_ref[pl.ds(2 * step, 2)]
    reach = reach_of(table, bounds[0:1, 0:1])
    reach = jnp.maximum(reach[0], reach[1]) * peak
    table = table.reshape(2 * length, 2 * length)
    for b in range(seqs):
        high, low = split(dot(table, grads[:, b * out_width : (b + 1) * out_width]) * (RANGE / reach))
        low = (low / matrix_scale.astype(F32)).astype(F8)
        for k in range(2):
            source, columns = slice(k * length, (k + 1) * length), slice(k * out_width, (k + 1) * out_width)
            parts[b * length : (b + 1) * length, columns] = high[source]
            parts8[b * length : (b + 1) * length, columns] = low[source]
    total[...] += (dot(parts[...], matrix) + dot(parts8[...], matrix8)) * (reach / RANGE)

    @pl.when(step == pl.num_programs(0) - 1)
    def _():
        summed = total[...]
        exponent = jnp.floor(jnp.log2(jnp.maximum(largest(summed), TINY))) + 1.0
        summed = summed * jnp.exp2(14.0 - exponent)
        block = out.shape[1] - 8
        turned = [] if block % 128 == 0 else [summed.T]
        for j in range(out.shape[0]):
            place = slice(j * block, (j + 1) * block)
            out[j, :block] = turned[0][place] if turned else summed[:, place].T
            out[j, block:] = jnp.broadcast_to(exponent, (8, tokens))


def back_sums(pieces, rows, matrices, cout):
    count, out_width, in_width = matrices.shape
    length = rows.shape[1]
    tokens = pieces[0].shape[1]
    seqs = tokens // length
    out = jax.ShapeDtypeStruct((cout, in_width // cout + 8, tokens), F32)
    return call(
        functools.partial(back_kernel, len(pieces)),
        (4 * count * out_width * in_width * tokens, 2 * matrices.size),
        32,
        out_shape=out,
        grid=(count // 2,),
        in_specs=[whole(piece) for piece in pieces]
        + [whole(rows), pl.BlockSpec((2, out_width, in_width), lambda i: (i, 0, 0))],
        out_specs=whole(out),
        scratch_shapes=[
            pltpu.VMEM((2 * length, seqs * out_width), BF16),
            pltpu.VMEM((tokens, 2 * out_width), BF16),
            pltpu.VMEM((tokens, 2 * out_width), F8),
            pltpu.VMEM((tokens, in_width), F32),
            pltpu.VMEM((8, length), F32),
        ],
    )(*pieces, rows, matrices)


def matrix_kernel(cin_count, input_count, cout_count, *refs):
    pieces = refs[:cin_count]
    input_pieces = refs[cin_count : cin_count + input_count]
    rows_ref, columns_ref, out_ref, grads, inputs, inputs8, parts, parts8, bounds = refs[cin_count + input_count :]
    step = pl.program_id(0)
    _, length, _ = rows_ref.shape
    tokens = inputs.shape[0]
    seqs = tokens // length
    out_width = out_ref.shape[1]

    @pl.when(step == 0)
    def _():
        block = pieces[0].shape[0]
        for r, piece in enumerate(pieces):
            for b in range(seqs):
                rows = spot("cin", r, block, cin_count, b * out_width)
                part = piece[:, b * length : (b + 1) * length]
                grads[rows, :length] = part
                grads[rows, length:] = part
        gmax = functools.reduce(jnp.maximum, [largest(piece[...]) for piece in pieces])
        xmax = functools.reduce(jnp.maximum, [largest(piece[half]) for piece in input_pieces for half in range(piece.shape[0])])
        xmax = jnp.maximum(xmax, TINY)
        bounds[0:1, :] = jnp.broadcast_to(gmax, (1, length))
        bounds[1:2, :] = jnp.broadcast_to(xmax, (1, length))
        block = input_pieces[0].shape[1]
        for r, piece in enumerate(input_pieces):
            for half in range(piece.shape[0]):
                columns = spot("cout", 2 * r + half, block, cout_count)
                turned = piece[half].astype(F32).T
                inputs[:, columns] = turned.astype(BF16)
                inputs8[:, columns] = (turned * (256.0 / xmax)).astype(F8)

    xmax = bounds[1:2, 0:1]
    reach = [bound * xmax for bound in reach_of(rows_ref[pl.ds(2 * step, 2)], bounds[0:1, 0:1])]
    table = columns_ref[step]
    for b in range(seqs):
        place = slice(b * length, (b + 1) * length)
        filtered = dot(grads[b * out_width : (b + 1) * out_width], table)
        for k in range(2):
            high, low = split(filtered[:, k * length : (k + 1) * length] * (RANGE / reach[k]))
            parts[k, :, place] = high
            parts8[k, :, place] = (low * (xmax / 256.0)).astype(F8)
    for k in range(2):
        total = dot(parts[k], inputs[...]) + dot(parts8[k], inputs8[...])
        out_ref[k] = (total * (reach[k] / RANGE)).astype(BF16)


def matrix_sums(pieces, input_pieces, rows, columns, cout_count, shape):
    count, out_width, in_width = shape
    length = rows.shape[1]
    tokens = pieces[0].shape[1]
    seqs = tokens // length
    return call(
        functools.partial(matrix_kernel, len(pieces), len(input_pieces), cout_count),
        (3 * count * out_width * in_width * tokens, 2 * count * out_width * in_width),
        32,
        out_shape=jax.ShapeDtypeStruct(shape, BF16),
        grid=(count // 2,),
        in_specs=[whole(piece) for piece in (*pieces, *input_pieces)] + [whole(rows), whole(columns)],
        out_specs=pl.BlockSpec((2, out_width, in_width), lambda i: (i, 0, 0)),
        scratch_shapes=[
            pltpu.VMEM((seqs * out_width, 2 * length), BF16),
            pltpu.VMEM((tokens, in_width), BF16),
            pltpu.VMEM((tokens, in_width), F8),
            pltpu.VMEM((2, out_width, tokens), BF16),
            pltpu.VMEM((2, out_width, tokens), F8),
            pltpu.VMEM((8, length), F32),
        ],
    )(*pieces, *input_pieces, rows, columns)


def exchange(array, axis, count, flip):
    return lax.ppermute(array, axis, [(i, i ^ flip) for i in range(count)])


def shards(cin, cout, inputs, cotangent, matrices, filters):
    own, seq_count, length = inputs.shape
    tokens = seq_count * length
    flat_grads = cotangent.reshape(-1, tokens)
    if cin & (cin - 1) or flat_grads.shape[0] % 128:
        pieces = [lax.all_gather(flat_grads, "cin", axis=0, tiled=True)]
    else:
        pieces = [flat_grads] + [exchange(flat_grads, "cin", cin, flip) for flip in range(1, cin)]
    rows, columns = make_tables(lax.optimization_barrier((filters, flat_grads))[0])
    flat_inputs = inputs.reshape(-1, tokens)
    if cout < 2 or cout & (cout - 1) or own % 128:
        input_pieces = [lax.all_gather(flat_inputs, "cout", axis=0, tiled=True)[None]]
        cout_count = 1
    else:
        both = jnp.concatenate([flat_inputs, exchange(flat_inputs, "cout", cout, 1)]).reshape(2, own, tokens)
        input_pieces = [both] + [exchange(both, "cout", cout, flip) for flip in range(2, cout, 2)]
        cout_count = cout

    blocks = back_sums(pieces, rows, matrices, cout).astype(F16)
    came = lax.all_to_all(blocks, "cout", 0, 0, tiled=True)
    matrix_grads = matrix_sums(pieces, input_pieces, rows, columns, cout_count, matrices.shape)
    scales = jnp.exp2(came[:, own : own + 1].astype(F32) - 14.0)
    input_grads = jnp.sum(came[:, :own].astype(F32) * scales, axis=0).astype(BF16)
    return (matrix_grads, input_grads.reshape(own, seq_count, length))


def solution(mesh):
    placed = (
        P(("cin", "cout"), None, None),
        P(("cout", "cin"), None, None),
        P(None, "cout", "cin"),
        P(),
    )
    return jax.shard_map(
        functools.partial(shards, mesh.shape["cin"], mesh.shape["cout"]),
        mesh=mesh,
        in_specs=placed,
        out_specs=(P(None, "cout", "cin"), P(("cin", "cout"), None, None)),
        check_vma=False,
    )
```

```python
import functools

import jax
import jax.numpy as jnp
from jax import lax
from jax.experimental import pallas as pl
from jax.experimental.pallas import tpu as pltpu
from jax.sharding import PartitionSpec as P

BF16 = jnp.bfloat16
F16 = jnp.float16
F32 = jnp.float32
F8 = jnp.float8_e4m3fn
MIB = 1024 * 1024
GROUP = 4
TINY = 1e-30


def split(wide):
    high = wide.astype(BF16)
    return high, wide - high.astype(F32)


def dot(left, right):
    return jnp.dot(left, right, preferred_element_type=F32)


def call(body, cost, limit, **kwargs):
    flops, moved = cost
    return pl.pallas_call(
        body,
        compiler_params=pltpu.CompilerParams(vmem_limit_bytes=limit * MIB),
        cost_estimate=pl.CostEstimate(flops=flops, bytes_accessed=moved, transcendentals=0),
        **kwargs,
    )


def whole(array):
    return pl.BlockSpec(array.shape, lambda i: (0,) * len(array.shape))


def largest(array):
    return jnp.max(jnp.abs(array.astype(F32)), keepdims=True)


def spot(axis, flip, block, count, base=0):
    if count == 1:
        return slice(base, base + block)
    return pl.ds(pl.multiple_of(base + (lax.axis_index(axis) ^ flip) * block, block), block)


def reach_of(table, gmax):
    length = table.shape[1]
    sums = [jnp.sum(jnp.abs(table[k, 0:1, :length].astype(F32)), keepdims=True) for k in range(table.shape[0])]
    return [jnp.maximum(total * gmax, TINY) for total in sums]


def table_kernel(filters_ref, rows_ref):
    count, length = filters_ref.shape
    source = lax.broadcasted_iota(jnp.int32, (length, length), 0)
    token = lax.broadcasted_iota(jnp.int32, (length, length), 1)
    for k in range(count):
        spread = jnp.broadcast_to(filters_ref[k : k + 1, :], (length, length))
        shifted = pltpu.roll(spread, 0, 1, stride=1, stride_axis=0)
        high, low = split(jnp.where(token >= source, shifted, 0.0))
        rows_ref[k, :, :length] = high
        rows_ref[k, :, length:] = low.astype(BF16)


def make_tables(filters):
    count, length = filters.shape
    return call(
        table_kernel,
        (count * length * length * 4, count * length * length * 4),
        8,
        out_shape=jax.ShapeDtypeStruct((count, length, 2 * length), BF16),
    )(filters)


def back_kernel(cin_count, *refs):
    pieces = refs[:cin_count]
    rows_ref, matrix_ref, out, grads, parts, parts8, total, bounds = refs[cin_count:]
    step = pl.program_id(0)
    _, length, _ = rows_ref.shape
    out_width = matrix_ref.shape[1]
    seqs = grads.shape[1] // out_width
    tokens = seqs * length

    @pl.when(step == 0)
    def _():
        total[...] = jnp.zeros_like(total)
        block = pieces[0].shape[0]
        for b in range(seqs):
            for r, piece in enumerate(pieces):
                turned = piece[:, b * length : (b + 1) * length].astype(F32).T.astype(BF16)
                columns = spot("cin", r, block, cin_count, b * out_width)
                grads[:length, columns] = turned
                grads[length:, columns] = turned
        gmax = functools.reduce(jnp.maximum, [largest(piece[...]) for piece in pieces])
        bounds[...] = jnp.broadcast_to(gmax, bounds.shape)

    matrix = matrix_ref[...].reshape(GROUP * out_width, -1)
    peak = jnp.max(jnp.abs(matrix).reshape(-1, 16, matrix.shape[1]), axis=0)
    matrix_scale = (256.0 / jnp.maximum(largest(peak), TINY)).astype(BF16)
    matrix8 = (matrix * matrix_scale).astype(F8)
    table = rows_ref[pl.ds(GROUP * step, GROUP)]
    reach = functools.reduce(jnp.maximum, reach_of(table, bounds[0:1, 0:1]))
    table = table.reshape(GROUP * length, 2 * length)
    for b in range(seqs):
        high, low = split(dot(table, grads[:, b * out_width : (b + 1) * out_width]))
        low = (low * (65536.0 / reach)).astype(F8)
        for k in range(GROUP):
            source, columns = slice(k * length, (k + 1) * length), slice(k * out_width, (k + 1) * out_width)
            parts[b * length : (b + 1) * length, columns] = high[source]
            parts8[b * length : (b + 1) * length, columns] = low[source]
    back = (reach / 65536.0) / matrix_scale.astype(F32)
    total[...] += dot(parts[...], matrix) + dot(parts8[...], matrix8) * back

    @pl.when(step == pl.num_programs(0) - 1)
    def _():
        summed = total[...]
        exponent = jnp.floor(jnp.log2(jnp.maximum(largest(summed), TINY))) + 1.0
        summed = summed * jnp.exp2(14.0 - exponent)
        block = out.shape[1] - 8
        turned = [] if block % 128 == 0 else [summed.T]
        for j in range(out.shape[0]):
            place = slice(j * block, (j + 1) * block)
            out[j, :block] = turned[0][place] if turned else summed[:, place].T
            out[j, block:] = jnp.broadcast_to(exponent, (8, tokens))


def back_sums(pieces, rows, matrices, cout):
    count, out_width, in_width = matrices.shape
    length = rows.shape[1]
    tokens = pieces[0].shape[1]
    seqs = tokens // length
    out = jax.ShapeDtypeStruct((cout, in_width // cout + 8, tokens), F32)
    return call(
        functools.partial(back_kernel, len(pieces)),
        (4 * count * out_width * in_width * tokens, 2 * matrices.size),
        40,
        out_shape=out,
        grid=(count // GROUP,),
        in_specs=[whole(piece) for piece in pieces]
        + [whole(rows), pl.BlockSpec((GROUP, out_width, in_width), lambda i: (i, 0, 0))],
        out_specs=whole(out),
        scratch_shapes=[
            pltpu.VMEM((2 * length, seqs * out_width), BF16),
            pltpu.VMEM((tokens, GROUP * out_width), BF16),
            pltpu.VMEM((tokens, GROUP * out_width), F8),
            pltpu.VMEM((tokens, in_width), F32),
            pltpu.VMEM((8, length), F32),
        ],
    )(*pieces, rows, matrices)


def matrix_kernel(cin_count, input_count, cout_count, *refs):
    pieces = refs[:cin_count]
    input_pieces = refs[cin_count : cin_count + input_count]
    rows_ref, out_ref, grads, inputs, inputs8, parts, parts8, bounds = refs[cin_count + input_count :]
    step = pl.program_id(0)
    _, length, _ = rows_ref.shape
    tokens = inputs.shape[0]
    seqs = tokens // length
    out_width = out_ref.shape[1]

    @pl.when(step == 0)
    def _():
        block = pieces[0].shape[0]
        for r, piece in enumerate(pieces):
            for b in range(seqs):
                rows = spot("cin", r, block, cin_count, b * out_width)
                part = piece[:, b * length : (b + 1) * length]
                grads[rows, :length] = part
                grads[rows, length:] = part
        gmax = functools.reduce(jnp.maximum, [largest(piece[...]) for piece in pieces])
        xmax = functools.reduce(jnp.maximum, [largest(piece[half]) for piece in input_pieces for half in range(piece.shape[0])])
        xmax = jnp.maximum(xmax, TINY)
        bounds[0:1, :] = jnp.broadcast_to(gmax, (1, length))
        bounds[1:2, :] = jnp.broadcast_to(xmax, (1, length))
        block = input_pieces[0].shape[1]
        for r, piece in enumerate(input_pieces):
            for half in range(piece.shape[0]):
                columns = spot("cout", 2 * r + half, block, cout_count)
                turned = piece[half].astype(F32).T
                inputs[:, columns] = turned.astype(BF16)
                inputs8[:, columns] = (turned * (256.0 / xmax)).astype(F8)

    table = rows_ref[pl.ds(GROUP * step, GROUP)]
    reach = reach_of(table, bounds[0:1, 0:1])
    table = table.reshape(GROUP * length, 2 * length)
    for first in range(0, GROUP, 2):
        some = table[first * length : (first + 2) * length]
        for b in range(seqs):
            place = slice(b * length, (b + 1) * length)
            filtered = lax.dot_general(
                grads[b * out_width : (b + 1) * out_width], some, (((1,), (1,)), ((), ())), preferred_element_type=F32
            )
            high, low = split(filtered)
            for k in range(2):
                columns = slice(k * length, (k + 1) * length)
                parts[first + k, :, place] = high[:, columns]
                parts8[first + k, :, place] = (low[:, columns] * (65536.0 / reach[first + k])).astype(F8)
    for k in range(GROUP):
        back = (reach[k] / 65536.0) * (bounds[1:2, 0:1] / 256.0)
        product = dot(parts[k], inputs[...]) + dot(parts8[k], inputs8[...]) * back
        out_ref[k] = product.astype(BF16)


def matrix_sums(pieces, input_pieces, rows, cout_count, shape):
    count, out_width, in_width = shape
    length = rows.shape[1]
    tokens = pieces[0].shape[1]
    seqs = tokens // length
    return call(
        functools.partial(matrix_kernel, len(pieces), len(input_pieces), cout_count),
        (3 * count * out_width * in_width * tokens, 2 * count * out_width * in_width),
        32,
        out_shape=jax.ShapeDtypeStruct(shape, BF16),
        grid=(count // GROUP,),
        in_specs=[whole(piece) for piece in (*pieces, *input_pieces)] + [whole(rows)],
        out_specs=pl.BlockSpec((GROUP, out_width, in_width), lambda i: (i, 0, 0)),
        scratch_shapes=[
            pltpu.VMEM((seqs * out_width, 2 * length), BF16),
            pltpu.VMEM((tokens, in_width), BF16),
            pltpu.VMEM((tokens, in_width), F8),
            pltpu.VMEM((GROUP, out_width, tokens), BF16),
            pltpu.VMEM((GROUP, out_width, tokens), F8),
            pltpu.VMEM((8, length), F32),
        ],
    )(*pieces, *input_pieces, rows)


def exchange(array, axis, count, flip):
    return lax.ppermute(array, axis, [(i, i ^ flip) for i in range(count)])


def shards(cin, cout, inputs, cotangent, matrices, filters):
    own, seq_count, length = inputs.shape
    tokens = seq_count * length
    flat_grads = cotangent.reshape(-1, tokens)
    if cin & (cin - 1) or flat_grads.shape[0] % 128:
        pieces = [lax.all_gather(flat_grads, "cin", axis=0, tiled=True)]
    else:
        pieces = [flat_grads] + [exchange(flat_grads, "cin", cin, flip) for flip in range(1, cin)]
    rows = make_tables(lax.optimization_barrier((filters, flat_grads))[0])
    flat_inputs = inputs.reshape(-1, tokens)
    if cout < 2 or cout & (cout - 1) or own % 128:
        input_pieces = [lax.all_gather(flat_inputs, "cout", axis=0, tiled=True)[None]]
        cout_count = 1
    else:
        both = jnp.concatenate([flat_inputs, exchange(flat_inputs, "cout", cout, 1)]).reshape(2, own, tokens)
        input_pieces = [both] + [exchange(both, "cout", cout, flip) for flip in range(2, cout, 2)]
        cout_count = cout

    blocks = back_sums(pieces, rows, matrices, cout).astype(F16)
    came = lax.all_to_all(blocks, "cout", 0, 0, tiled=True)
    matrix_grads = matrix_sums(pieces, input_pieces, rows, cout_count, matrices.shape)
    scales = jnp.exp2(came[:, own : own + 1].astype(F32) - 14.0)
    input_grads = jnp.sum(came[:, :own].astype(F32) * scales, axis=0).astype(BF16)
    return (matrix_grads, input_grads.reshape(own, seq_count, length))


def solution(mesh):
    placed = (
        P(("cin", "cout"), None, None),
        P(("cout", "cin"), None, None),
        P(None, "cout", "cin"),
        P(),
    )
    return jax.shard_map(
        functools.partial(shards, mesh.shape["cin"], mesh.shape["cout"]),
        mesh=mesh,
        in_specs=placed,
        out_specs=(P(None, "cout", "cin"), P(("cin", "cout"), None, None)),
        check_vma=False,
    )
```

```python
import functools
import itertools

import jax
import jax.numpy as jnp
from jax import lax
from jax.experimental import pallas as pl
from jax.experimental.pallas import tpu as pltpu
from jax.sharding import PartitionSpec as P

BF16 = jnp.bfloat16
F16 = jnp.float16
F32 = jnp.float32
F8 = jnp.float8_e4m3fn
MIB = 1024 * 1024
GROUP = 4
CHUNK = 256
TINY = 1e-30


def split(wide):
    high = wide.astype(BF16)
    return high, wide - high.astype(F32)


def dot(left, right):
    return jnp.dot(left, right, preferred_element_type=F32)


def call(body, cost, limit, **kwargs):
    flops, moved = cost
    return pl.pallas_call(
        body,
        compiler_params=pltpu.CompilerParams(vmem_limit_bytes=limit * MIB),
        cost_estimate=pl.CostEstimate(flops=flops, bytes_accessed=moved, transcendentals=0),
        **kwargs,
    )


def whole(array):
    return pl.BlockSpec(array.shape, lambda i: (0,) * len(array.shape))


def largest(array):
    return jnp.max(jnp.abs(array.astype(F32)), keepdims=True)


def spot(axis, flip, block, count, base=0):
    if count == 1:
        return slice(base, base + block)
    return pl.ds(pl.multiple_of(base + (lax.axis_index(axis) ^ flip) * block, block), block)


def reach_of(table, gmax):
    length = table.shape[1]
    sums = [jnp.sum(jnp.abs(table[k, 0:1, :length].astype(F32)), keepdims=True) for k in range(table.shape[0])]
    return [jnp.maximum(total * gmax, TINY) for total in sums]


def interleave(first, second):
    for one, other in itertools.zip_longest(first, second):
        for work in (one, other):
            if work is not None:
                work()


def chunks(width):
    size = min(width, CHUNK)
    return [slice(start, start + size) for start in range(0, width, size)]


def table_kernel(filters_ref, rows_ref):
    count, length = filters_ref.shape
    source = lax.broadcasted_iota(jnp.int32, (length, length), 0)
    token = lax.broadcasted_iota(jnp.int32, (length, length), 1)
    for k in range(count):
        spread = jnp.broadcast_to(filters_ref[k : k + 1, :], (length, length))
        shifted = pltpu.roll(spread, 0, 1, stride=1, stride_axis=0)
        high, low = split(jnp.where(token >= source, shifted, 0.0))
        rows_ref[k, :, :length] = high
        rows_ref[k, :, length:] = low.astype(BF16)


def make_tables(filters):
    count, length = filters.shape
    return call(
        table_kernel,
        (count * length * length * 4, count * length * length * 4),
        8,
        out_shape=jax.ShapeDtypeStruct((count, length, 2 * length), BF16),
    )(filters)


def back_kernel(cin_count, *refs):
    pieces = refs[:cin_count]
    rows_ref, matrix_ref, out, grads, parts, parts8, total, bounds = refs[cin_count:]
    step = pl.program_id(0)
    _, length, _ = rows_ref.shape
    out_width = matrix_ref.shape[1]
    seqs = grads.shape[1] // out_width
    tokens = seqs * length

    def table_of(first):
        table = rows_ref[pl.ds(first, 2)]
        reach = functools.reduce(jnp.maximum, reach_of(table, bounds[0:1, 0:1]))
        return table.reshape(2 * length, 2 * length), reach

    def filter_sequence(slot, table, reach, b):
        high, low = split(dot(table, grads[:, b * out_width : (b + 1) * out_width]))
        low = (low * (65536.0 / reach)).astype(F8)
        rows = slice(b * length, (b + 1) * length)
        for k in range(2):
            source, columns = slice(k * length, (k + 1) * length), slice(k * out_width, (k + 1) * out_width)
            parts[slot, rows, columns] = high[source]
            parts8[slot, rows, columns] = low[source]

    def filters_of(slot, table, reach):
        return [functools.partial(filter_sequence, slot, table, reach, b) for b in range(seqs)]

    @pl.when(step == 0)
    def _():
        total[...] = jnp.zeros_like(total)
        block = pieces[0].shape[0]
        for b in range(seqs):
            for r, piece in enumerate(pieces):
                turned = piece[:, b * length : (b + 1) * length].astype(F32).T.astype(BF16)
                columns = spot("cin", r, block, cin_count, b * out_width)
                grads[:length, columns] = turned
                grads[length:, columns] = turned
        gmax = functools.reduce(jnp.maximum, [largest(piece[...]) for piece in pieces])
        bounds[...] = jnp.broadcast_to(gmax, bounds.shape)
        interleave(filters_of(0, *table_of(0)), [])

    peak = jnp.max(jnp.abs(matrix_ref[...]).reshape(-1, 16, matrix_ref.shape[2]), axis=0)
    matrix_scale = (256.0 / jnp.maximum(largest(peak), TINY)).astype(BF16)

    def product(slot, back, columns):
        matrix = matrix_ref[2 * slot : 2 * slot + 2, :, columns].reshape(2 * out_width, -1)
        matrix8 = (matrix * matrix_scale).astype(F8)
        total[:, columns] += dot(parts[slot], matrix) + dot(parts8[slot], matrix8) * back

    def products_of(slot, reach):
        back = (reach / 65536.0) / matrix_scale.astype(F32)
        return [functools.partial(product, slot, back, columns) for columns in chunks(matrix_ref.shape[2])]

    now = table_of(GROUP * step)
    late = table_of(GROUP * step + 2)
    coming = table_of(lax.rem(GROUP * step + GROUP, rows_ref.shape[0]))
    interleave(products_of(0, now[1]), filters_of(1, *late))
    interleave(products_of(1, late[1]), filters_of(0, *coming))

    @pl.when(step == pl.num_programs(0) - 1)
    def _():
        summed = total[...]
        exponent = jnp.floor(jnp.log2(jnp.maximum(largest(summed), TINY))) + 1.0
        summed = summed * jnp.exp2(14.0 - exponent)
        block = out.shape[1] - 8
        turned = [] if block % 128 == 0 else [summed.T]
        for j in range(out.shape[0]):
            place = slice(j * block, (j + 1) * block)
            out[j, :block] = turned[0][place] if turned else summed[:, place].T
            out[j, block:] = jnp.broadcast_to(exponent, (8, tokens))


def back_sums(pieces, rows, matrices, cout):
    count, out_width, in_width = matrices.shape
    length = rows.shape[1]
    tokens = pieces[0].shape[1]
    seqs = tokens // length
    out = jax.ShapeDtypeStruct((cout, in_width // cout + 8, tokens), F32)
    return call(
        functools.partial(back_kernel, len(pieces)),
        (4 * count * out_width * in_width * tokens, 2 * matrices.size),
        40,
        out_shape=out,
        grid=(count // GROUP,),
        in_specs=[whole(piece) for piece in pieces]
        + [whole(rows), pl.BlockSpec((GROUP, out_width, in_width), lambda i: (i, 0, 0))],
        out_specs=whole(out),
        scratch_shapes=[
            pltpu.VMEM((2 * length, seqs * out_width), BF16),
            pltpu.VMEM((2, tokens, 2 * out_width), BF16),
            pltpu.VMEM((2, tokens, 2 * out_width), F8),
            pltpu.VMEM((tokens, in_width), F32),
            pltpu.VMEM((8, length), F32),
        ],
    )(*pieces, rows, matrices)


def matrix_kernel(cin_count, input_count, cout_count, *refs):
    pieces = refs[:cin_count]
    input_pieces = refs[cin_count : cin_count + input_count]
    rows_ref, out_ref, grads, inputs, inputs8, parts, parts8, bounds = refs[cin_count + input_count :]
    step = pl.program_id(0)
    _, length, _ = rows_ref.shape
    tokens = inputs.shape[0]
    seqs = tokens // length
    out_width = out_ref.shape[1]

    def table_of(first):
        table = rows_ref[pl.ds(first, 2)]
        return table.reshape(2 * length, 2 * length), reach_of(table, bounds[0:1, 0:1])

    def filter_sequence(slot, table, reach, b):
        filtered = lax.dot_general(
            grads[b * out_width : (b + 1) * out_width], table, (((1,), (1,)), ((), ())), preferred_element_type=F32
        )
        high, low = split(filtered)
        place = slice(b * length, (b + 1) * length)
        for k in range(2):
            columns = slice(k * length, (k + 1) * length)
            parts[2 * slot + k, :, place] = high[:, columns]
            parts8[2 * slot + k, :, place] = (low[:, columns] * (65536.0 / reach[k])).astype(F8)

    def filters_of(slot, table, reach):
        return [functools.partial(filter_sequence, slot, table, reach, b) for b in range(seqs)]

    def product(k, back, columns):
        total = dot(parts[k], inputs[:, columns]) + dot(parts8[k], inputs8[:, columns]) * back
        out_ref[k, :, columns] = total.astype(BF16)

    def products_of(slot, reach):
        backs = [(reach[k] / 65536.0) * (bounds[1:2, 0:1] / 256.0) for k in range(2)]
        return [
            functools.partial(product, 2 * slot + k, backs[k], columns)
            for k in range(2)
            for columns in chunks(inputs.shape[1])
        ]

    @pl.when(step == 0)
    def _():
        block = pieces[0].shape[0]
        for r, piece in enumerate(pieces):
            for b in range(seqs):
                rows = spot("cin", r, block, cin_count, b * out_width)
                part = piece[:, b * length : (b + 1) * length]
                grads[rows, :length] = part
                grads[rows, length:] = part
        gmax = functools.reduce(jnp.maximum, [largest(piece[...]) for piece in pieces])
        xmax = functools.reduce(jnp.maximum, [largest(piece[half]) for piece in input_pieces for half in range(piece.shape[0])])
        xmax = jnp.maximum(xmax, TINY)
        bounds[0:1, :] = jnp.broadcast_to(gmax, (1, length))
        bounds[1:2, :] = jnp.broadcast_to(xmax, (1, length))
        block = input_pieces[0].shape[1]
        for r, piece in enumerate(input_pieces):
            for half in range(piece.shape[0]):
                columns = spot("cout", 2 * r + half, block, cout_count)
                turned = piece[half].astype(F32).T
                inputs[:, columns] = turned.astype(BF16)
                inputs8[:, columns] = (turned * (256.0 / xmax)).astype(F8)
        interleave(filters_of(0, *table_of(0)), [])

    now = table_of(GROUP * step)
    late = table_of(GROUP * step + 2)
    coming = table_of(lax.rem(GROUP * step + GROUP, rows_ref.shape[0]))
    interleave(products_of(0, now[1]), filters_of(1, *late))
    interleave(products_of(1, late[1]), filters_of(0, *coming))


def matrix_sums(pieces, input_pieces, rows, cout_count, shape):
    count, out_width, in_width = shape
    length = rows.shape[1]
    tokens = pieces[0].shape[1]
    seqs = tokens // length
    return call(
        functools.partial(matrix_kernel, len(pieces), len(input_pieces), cout_count),
        (3 * count * out_width * in_width * tokens, 2 * count * out_width * in_width),
        32,
        out_shape=jax.ShapeDtypeStruct(shape, BF16),
        grid=(count // GROUP,),
        in_specs=[whole(piece) for piece in (*pieces, *input_pieces)] + [whole(rows)],
        out_specs=pl.BlockSpec((GROUP, out_width, in_width), lambda i: (i, 0, 0)),
        scratch_shapes=[
            pltpu.VMEM((seqs * out_width, 2 * length), BF16),
            pltpu.VMEM((tokens, in_width), BF16),
            pltpu.VMEM((tokens, in_width), F8),
            pltpu.VMEM((GROUP, out_width, tokens), BF16),
            pltpu.VMEM((GROUP, out_width, tokens), F8),
            pltpu.VMEM((8, length), F32),
        ],
    )(*pieces, *input_pieces, rows)


def exchange(array, axis, count, flip):
    return lax.ppermute(array, axis, [(i, i ^ flip) for i in range(count)])


def shards(cin, cout, inputs, cotangent, matrices, filters):
    own, seq_count, length = inputs.shape
    tokens = seq_count * length
    flat_grads = cotangent.reshape(-1, tokens)
    if cin & (cin - 1) or flat_grads.shape[0] % 128:
        pieces = [lax.all_gather(flat_grads, "cin", axis=0, tiled=True)]
    else:
        pieces = [flat_grads] + [exchange(flat_grads, "cin", cin, flip) for flip in range(1, cin)]
    rows = make_tables(lax.optimization_barrier((filters, flat_grads))[0])
    flat_inputs = inputs.reshape(-1, tokens)
    if cout < 2 or cout & (cout - 1) or own % 128:
        input_pieces = [lax.all_gather(flat_inputs, "cout", axis=0, tiled=True)[None]]
        cout_count = 1
    else:
        both = jnp.concatenate([flat_inputs, exchange(flat_inputs, "cout", cout, 1)]).reshape(2, own, tokens)
        input_pieces = [both] + [exchange(both, "cout", cout, flip) for flip in range(2, cout, 2)]
        cout_count = cout

    blocks = back_sums(pieces, rows, matrices, cout).astype(F16)
    came = lax.all_to_all(blocks, "cout", 0, 0, tiled=True)
    matrix_grads = matrix_sums(pieces, input_pieces, rows, cout_count, matrices.shape)
    scales = jnp.exp2(came[:, own : own + 1].astype(F32) - 14.0)
    input_grads = jnp.sum(came[:, :own].astype(F32) * scales, axis=0).astype(BF16)
    return (matrix_grads, input_grads.reshape(own, seq_count, length))


def solution(mesh):
    placed = (
        P(("cin", "cout"), None, None),
        P(("cout", "cin"), None, None),
        P(None, "cout", "cin"),
        P(),
    )
    return jax.shard_map(
        functools.partial(shards, mesh.shape["cin"], mesh.shape["cout"]),
        mesh=mesh,
        in_specs=placed,
        out_specs=(P(None, "cout", "cin"), P(("cin", "cout"), None, None)),
        check_vma=False,
    )
```

```python
import functools
import itertools

import jax
import jax.numpy as jnp
from jax import lax
from jax.experimental import pallas as pl
from jax.experimental.pallas import tpu as pltpu
from jax.sharding import PartitionSpec as P

BF16 = jnp.bfloat16
F16 = jnp.float16
F32 = jnp.float32
F8 = jnp.float8_e4m3fn
MIB = 1024 * 1024
GROUP = 4
CHUNK = 256
TINY = 1e-30


def split(wide):
    high = wide.astype(BF16)
    return high, wide - high.astype(F32)


def dot(left, right):
    return jnp.dot(left, right, preferred_element_type=F32)


def call(body, cost, limit, **kwargs):
    flops, moved = cost
    return pl.pallas_call(
        body,
        compiler_params=pltpu.CompilerParams(vmem_limit_bytes=limit * MIB),
        cost_estimate=pl.CostEstimate(flops=flops, bytes_accessed=moved, transcendentals=0),
        **kwargs,
    )


def whole(array):
    return pl.BlockSpec(array.shape, lambda i: (0,) * len(array.shape))


def largest(array):
    return jnp.max(jnp.abs(array.astype(F32)), keepdims=True)


def spot(axis, flip, block, count, base=0):
    if count == 1:
        return slice(base, base + block)
    return pl.ds(pl.multiple_of(base + (lax.axis_index(axis) ^ flip) * block, block), block)


def reach_of(table, gmax):
    length = table.shape[1]
    sums = [jnp.sum(jnp.abs(table[k, 0:1, :length].astype(F32)), keepdims=True) for k in range(table.shape[0])]
    return [jnp.maximum(total * gmax, TINY) for total in sums]


def interleave(first, second):
    for one, other in itertools.zip_longest(first, second):
        for work in (one, other):
            if work is not None:
                work()


def chunks(width):
    size = min(width, CHUNK)
    return [slice(start, start + size) for start in range(0, width, size)]


def table_kernel(filters_ref, rows_ref):
    count, length = filters_ref.shape
    source = lax.broadcasted_iota(jnp.int32, (length, length), 0)
    token = lax.broadcasted_iota(jnp.int32, (length, length), 1)
    for k in range(count):
        spread = jnp.broadcast_to(filters_ref[k : k + 1, :], (length, length))
        shifted = pltpu.roll(spread, 0, 1, stride=1, stride_axis=0)
        high, low = split(jnp.where(token >= source, shifted, 0.0))
        rows_ref[k, :, :length] = high
        rows_ref[k, :, length:] = low.astype(BF16)


def make_tables(filters):
    count, length = filters.shape
    return call(
        table_kernel,
        (count * length * length * 4, count * length * length * 4),
        8,
        out_shape=jax.ShapeDtypeStruct((count, length, 2 * length), BF16),
    )(filters)


def back_kernel(cin_count, *refs):
    pieces = refs[:cin_count]
    rows_ref, matrices_ref, out, grads, parts, parts8, total, bounds, blocks, arrived = refs[cin_count:]
    step = pl.program_id(0)
    slot = lax.rem(step, 2)
    _, length, _ = rows_ref.shape
    out_width = matrices_ref.shape[1]
    seqs = grads.shape[1] // out_width
    tokens = seqs * length

    def fetch(index):
        target = lax.rem(index, 2)
        return pltpu.make_async_copy(matrices_ref.at[pl.ds(GROUP * index, GROUP)], blocks.at[target], arrived.at[target])

    @pl.when(step == 0)
    def _():
        fetch(step).start()
        total[...] = jnp.zeros_like(total)
        block = pieces[0].shape[0]
        for b in range(seqs):
            for r, piece in enumerate(pieces):
                turned = piece[:, b * length : (b + 1) * length].astype(F32).T.astype(BF16)
                columns = spot("cin", r, block, cin_count, b * out_width)
                grads[:length, columns] = turned
                grads[length:, columns] = turned
        gmax = functools.reduce(jnp.maximum, [largest(piece[...]) for piece in pieces])
        bounds[...] = jnp.broadcast_to(gmax, bounds.shape)

    @pl.when(step + 1 < pl.num_programs(0))
    def _():
        fetch(step + 1).start()

    fetch(step).wait()
    matrix = blocks[slot].reshape(GROUP * out_width, -1)
    peak = jnp.max(jnp.abs(matrix).reshape(-1, 16, matrix.shape[1]), axis=0)
    matrix_scale = (256.0 / jnp.maximum(largest(peak), TINY)).astype(BF16)
    table = rows_ref[pl.ds(GROUP * step, GROUP)]
    reach = functools.reduce(jnp.maximum, reach_of(table, bounds[0:1, 0:1]))
    table = table.reshape(GROUP * length, 2 * length)
    for b in range(seqs):
        high, low = split(dot(table, grads[:, b * out_width : (b + 1) * out_width]))
        low = (low * (65536.0 / reach)).astype(F8)
        for k in range(GROUP):
            source, columns = slice(k * length, (k + 1) * length), slice(k * out_width, (k + 1) * out_width)
            parts[b * length : (b + 1) * length, columns] = high[source]
            parts8[b * length : (b + 1) * length, columns] = low[source]
    back = (reach / 65536.0) / matrix_scale.astype(F32)
    for columns in chunks(total.shape[1]):
        matrix = blocks[slot, :, :, columns].reshape(GROUP * out_width, -1)
        matrix8 = (matrix * matrix_scale).astype(F8)
        total[:, columns] += dot(parts[...], matrix) + dot(parts8[...], matrix8) * back

    @pl.when(step == pl.num_programs(0) - 1)
    def _():
        summed = total[...]
        exponent = jnp.floor(jnp.log2(jnp.maximum(largest(summed), TINY))) + 1.0
        summed = summed * jnp.exp2(14.0 - exponent)
        block = out.shape[1] - 8
        turned = [] if block % 128 == 0 else [summed.T]
        for j in range(out.shape[0]):
            place = slice(j * block, (j + 1) * block)
            out[j, :block] = turned[0][place] if turned else summed[:, place].T
            out[j, block:] = jnp.broadcast_to(exponent, (8, tokens))


def back_sums(pieces, rows, matrices, cout):
    count, out_width, in_width = matrices.shape
    length = rows.shape[1]
    tokens = pieces[0].shape[1]
    seqs = tokens // length
    out = jax.ShapeDtypeStruct((cout, in_width // cout + 8, tokens), F32)
    return call(
        functools.partial(back_kernel, len(pieces)),
        (4 * count * out_width * in_width * tokens, 2 * matrices.size),
        40,
        out_shape=out,
        grid=(count // GROUP,),
        in_specs=[whole(piece) for piece in pieces]
        + [whole(rows), pl.BlockSpec(memory_space=pl.ANY)],
        out_specs=whole(out),
        scratch_shapes=[
            pltpu.VMEM((2 * length, seqs * out_width), BF16),
            pltpu.VMEM((tokens, GROUP * out_width), BF16),
            pltpu.VMEM((tokens, GROUP * out_width), F8),
            pltpu.VMEM((tokens, in_width), F32),
            pltpu.VMEM((8, length), F32),
            pltpu.VMEM((2, GROUP, out_width, in_width), BF16),
            pltpu.SemaphoreType.DMA((2,)),
        ],
    )(*pieces, rows, matrices)


def matrix_kernel(cin_count, input_count, cout_count, *refs):
    pieces = refs[:cin_count]
    input_pieces = refs[cin_count : cin_count + input_count]
    rows_ref, out_ref, grads, inputs, inputs8, parts, parts8, bounds = refs[cin_count + input_count :]
    step = pl.program_id(0)
    _, length, _ = rows_ref.shape
    tokens = inputs.shape[0]
    seqs = tokens // length
    out_width = out_ref.shape[1]

    def table_of(first):
        table = rows_ref[pl.ds(first, 2)]
        return table.reshape(2 * length, 2 * length), reach_of(table, bounds[0:1, 0:1])

    def filter_sequence(slot, table, reach, b):
        filtered = lax.dot_general(
            grads[b * out_width : (b + 1) * out_width], table, (((1,), (1,)), ((), ())), preferred_element_type=F32
        )
        high, low = split(filtered)
        place = slice(b * length, (b + 1) * length)
        for k in range(2):
            columns = slice(k * length, (k + 1) * length)
            parts[2 * slot + k, :, place] = high[:, columns]
            parts8[2 * slot + k, :, place] = (low[:, columns] * (65536.0 / reach[k])).astype(F8)

    def filters_of(slot, table, reach):
        return [functools.partial(filter_sequence, slot, table, reach, b) for b in range(seqs)]

    def product(k, back, columns):
        total = dot(parts[k], inputs[:, columns]) + dot(parts8[k], inputs8[:, columns]) * back
        out_ref[k, :, columns] = total.astype(BF16)

    def products_of(slot, reach):
        backs = [(reach[k] / 65536.0) * (bounds[1:2, 0:1] / 256.0) for k in range(2)]
        return [
            functools.partial(product, 2 * slot + k, backs[k], columns)
            for k in range(2)
            for columns in chunks(inputs.shape[1])
        ]

    @pl.when(step == 0)
    def _():
        block = pieces[0].shape[0]
        for r, piece in enumerate(pieces):
            for b in range(seqs):
                rows = spot("cin", r, block, cin_count, b * out_width)
                part = piece[:, b * length : (b + 1) * length]
                grads[rows, :length] = part
                grads[rows, length:] = part
        gmax = functools.reduce(jnp.maximum, [largest(piece[...]) for piece in pieces])
        xmax = functools.reduce(jnp.maximum, [largest(piece[half]) for piece in input_pieces for half in range(piece.shape[0])])
        xmax = jnp.maximum(xmax, TINY)
        bounds[0:1, :] = jnp.broadcast_to(gmax, (1, length))
        bounds[1:2, :] = jnp.broadcast_to(xmax, (1, length))
        block = input_pieces[0].shape[1]
        for r, piece in enumerate(input_pieces):
            for half in range(piece.shape[0]):
                columns = spot("cout", 2 * r + half, block, cout_count)
                turned = piece[half].astype(F32).T
                inputs[:, columns] = turned.astype(BF16)
                inputs8[:, columns] = (turned * (256.0 / xmax)).astype(F8)
        interleave(filters_of(0, *table_of(0)), [])

    now = table_of(GROUP * step)
    late = table_of(GROUP * step + 2)
    coming = table_of(lax.rem(GROUP * step + GROUP, rows_ref.shape[0]))
    interleave(products_of(0, now[1]), filters_of(1, *late))
    interleave(products_of(1, late[1]), filters_of(0, *coming))


def matrix_sums(pieces, input_pieces, rows, cout_count, shape):
    count, out_width, in_width = shape
    length = rows.shape[1]
    tokens = pieces[0].shape[1]
    seqs = tokens // length
    return call(
        functools.partial(matrix_kernel, len(pieces), len(input_pieces), cout_count),
        (3 * count * out_width * in_width * tokens, 2 * count * out_width * in_width),
        32,
        out_shape=jax.ShapeDtypeStruct(shape, BF16),
        grid=(count // GROUP,),
        in_specs=[whole(piece) for piece in (*pieces, *input_pieces)] + [whole(rows)],
        out_specs=pl.BlockSpec((GROUP, out_width, in_width), lambda i: (i, 0, 0)),
        scratch_shapes=[
            pltpu.VMEM((seqs * out_width, 2 * length), BF16),
            pltpu.VMEM((tokens, in_width), BF16),
            pltpu.VMEM((tokens, in_width), F8),
            pltpu.VMEM((GROUP, out_width, tokens), BF16),
            pltpu.VMEM((GROUP, out_width, tokens), F8),
            pltpu.VMEM((8, length), F32),
        ],
    )(*pieces, *input_pieces, rows)


def exchange(array, axis, count, flip):
    return lax.ppermute(array, axis, [(i, i ^ flip) for i in range(count)])


def shards(cin, cout, inputs, cotangent, matrices, filters):
    own, seq_count, length = inputs.shape
    tokens = seq_count * length
    flat_grads = cotangent.reshape(-1, tokens)
    if cin & (cin - 1) or flat_grads.shape[0] % 128:
        pieces = [lax.all_gather(flat_grads, "cin", axis=0, tiled=True)]
    else:
        pieces = [flat_grads] + [exchange(flat_grads, "cin", cin, flip) for flip in range(1, cin)]
    rows = make_tables(lax.optimization_barrier((filters, flat_grads))[0])
    flat_inputs = inputs.reshape(-1, tokens)
    if cout < 2 or cout & (cout - 1) or own % 128:
        input_pieces = [lax.all_gather(flat_inputs, "cout", axis=0, tiled=True)[None]]
        cout_count = 1
    else:
        both = jnp.concatenate([flat_inputs, exchange(flat_inputs, "cout", cout, 1)]).reshape(2, own, tokens)
        input_pieces = [both] + [exchange(both, "cout", cout, flip) for flip in range(2, cout, 2)]
        cout_count = cout

    blocks = back_sums(pieces, rows, matrices, cout).astype(F16)
    came = lax.all_to_all(blocks, "cout", 0, 0, tiled=True)
    matrix_grads = matrix_sums(pieces, input_pieces, rows, cout_count, matrices.shape)
    scales = jnp.exp2(came[:, own : own + 1].astype(F32) - 14.0)
    input_grads = jnp.sum(came[:, :own].astype(F32) * scales, axis=0).astype(BF16)
    return (matrix_grads, input_grads.reshape(own, seq_count, length))


def solution(mesh):
    placed = (
        P(("cin", "cout"), None, None),
        P(("cout", "cin"), None, None),
        P(None, "cout", "cin"),
        P(),
    )
    return jax.shard_map(
        functools.partial(shards, mesh.shape["cin"], mesh.shape["cout"]),
        mesh=mesh,
        in_specs=placed,
        out_specs=(P(None, "cout", "cin"), P(("cin", "cout"), None, None)),
        check_vma=False,
    )
```

```python
import functools

import jax
import jax.numpy as jnp
from jax import lax
from jax.experimental import pallas as pl
from jax.experimental.pallas import tpu as pltpu
from jax.sharding import PartitionSpec as P

BF16 = jnp.bfloat16
F16 = jnp.float16
F32 = jnp.float32
F8 = jnp.float8_e4m3fn
MIB = 1024 * 1024
BACK_GROUP = 6
GROUP = 4
TINY = 1e-30


def split(wide):
    high = wide.astype(BF16)
    return high, wide - high.astype(F32)


def dot(left, right):
    return jnp.dot(left, right, preferred_element_type=F32)


def call(body, cost, limit, **kwargs):
    flops, moved = cost
    return pl.pallas_call(
        body,
        compiler_params=pltpu.CompilerParams(vmem_limit_bytes=limit * MIB),
        cost_estimate=pl.CostEstimate(flops=flops, bytes_accessed=moved, transcendentals=0),
        **kwargs,
    )


def whole(array):
    return pl.BlockSpec(array.shape, lambda i: (0,) * len(array.shape))


def largest(array):
    return jnp.max(jnp.abs(array.astype(F32)), keepdims=True)


def spot(axis, flip, block, count, base=0):
    if count == 1:
        return slice(base, base + block)
    return pl.ds(pl.multiple_of(base + (lax.axis_index(axis) ^ flip) * block, block), block)


def reach_of(table, gmax):
    length = table.shape[1]
    sums = [jnp.sum(jnp.abs(table[k, 0:1, :length].astype(F32)), keepdims=True) for k in range(table.shape[0])]
    return [jnp.maximum(total * gmax, TINY) for total in sums]


def interleave(first, second):
    ratio = -(-len(first) // len(second))
    for i, work in enumerate(second):
        for earlier in first[i * ratio : (i + 1) * ratio]:
            earlier()
        work()


def table_kernel(filters_ref, rows_ref):
    count, length = filters_ref.shape
    source = lax.broadcasted_iota(jnp.int32, (length, length), 0)
    token = lax.broadcasted_iota(jnp.int32, (length, length), 1)
    for k in range(count):
        spread = jnp.broadcast_to(filters_ref[k : k + 1, :], (length, length))
        shifted = pltpu.roll(spread, 0, 1, stride=1, stride_axis=0)
        high, low = split(jnp.where(token >= source, shifted, 0.0))
        rows_ref[k, :, :length] = high
        rows_ref[k, :, length:] = low.astype(BF16)


def make_tables(filters):
    count, length = filters.shape
    return call(
        table_kernel,
        (count * length * length * 4, count * length * length * 4),
        8,
        out_shape=jax.ShapeDtypeStruct((count, length, 2 * length), BF16),
    )(filters)


def back_kernel(cin_count, *refs):
    pieces = refs[:cin_count]
    rows_ref, matrix_ref, out, grads, parts, parts8, total, bounds = refs[cin_count:]
    step = pl.program_id(0)
    _, length, _ = rows_ref.shape
    out_width = matrix_ref.shape[1]
    seqs = grads.shape[1] // out_width
    tokens = seqs * length

    @pl.when(step == 0)
    def _():
        total[...] = jnp.zeros_like(total)
        block = pieces[0].shape[0]
        for b in range(seqs):
            for r, piece in enumerate(pieces):
                turned = piece[:, b * length : (b + 1) * length].astype(F32).T.astype(BF16)
                columns = spot("cin", r, block, cin_count, b * out_width)
                grads[:length, columns] = turned
                grads[length:, columns] = turned
        gmax = functools.reduce(jnp.maximum, [largest(piece[...]) for piece in pieces])
        bounds[...] = jnp.broadcast_to(gmax, bounds.shape)

    matrix = matrix_ref[...].reshape(BACK_GROUP * out_width, -1)
    peak = jnp.max(jnp.abs(matrix).reshape(-1, 16, matrix.shape[1]), axis=0)
    matrix_scale = (256.0 / jnp.maximum(largest(peak), TINY)).astype(BF16)
    matrix8 = (matrix * matrix_scale).astype(F8)
    table = rows_ref[pl.ds(BACK_GROUP * step, BACK_GROUP)]
    reach = functools.reduce(jnp.maximum, reach_of(table, bounds[0:1, 0:1]))
    table = table.reshape(BACK_GROUP * length, 2 * length)
    for b in range(seqs):
        high, low = split(dot(table, grads[:, b * out_width : (b + 1) * out_width]))
        low = (low * (65536.0 / reach)).astype(F8)
        for k in range(BACK_GROUP):
            source, columns = slice(k * length, (k + 1) * length), slice(k * out_width, (k + 1) * out_width)
            parts[b * length : (b + 1) * length, columns] = high[source]
            parts8[b * length : (b + 1) * length, columns] = low[source]
    back = (reach / 65536.0) / matrix_scale.astype(F32)
    total[...] += dot(parts[...], matrix) + dot(parts8[...], matrix8) * back

    @pl.when(step == pl.num_programs(0) - 1)
    def _():
        summed = total[...]
        exponent = jnp.floor(jnp.log2(jnp.maximum(largest(summed), TINY))) + 1.0
        summed = summed * jnp.exp2(14.0 - exponent)
        block = out.shape[1] - 8
        turned = [] if block % 128 == 0 else [summed.T]
        for j in range(out.shape[0]):
            place = slice(j * block, (j + 1) * block)
            out[j, :block] = turned[0][place] if turned else summed[:, place].T
            out[j, block:] = jnp.broadcast_to(exponent, (8, tokens))


def back_sums(pieces, rows, matrices, cout):
    count, out_width, in_width = matrices.shape
    length = rows.shape[1]
    tokens = pieces[0].shape[1]
    seqs = tokens // length
    out = jax.ShapeDtypeStruct((cout, in_width // cout + 8, tokens), F32)
    return call(
        functools.partial(back_kernel, len(pieces)),
        (4 * count * out_width * in_width * tokens, 2 * matrices.size),
        48,
        out_shape=out,
        grid=(count // BACK_GROUP,),
        in_specs=[whole(piece) for piece in pieces]
        + [whole(rows), pl.BlockSpec((BACK_GROUP, out_width, in_width), lambda i: (i, 0, 0))],
        out_specs=whole(out),
        scratch_shapes=[
            pltpu.VMEM((2 * length, seqs * out_width), BF16),
            pltpu.VMEM((tokens, BACK_GROUP * out_width), BF16),
            pltpu.VMEM((tokens, BACK_GROUP * out_width), F8),
            pltpu.VMEM((tokens, in_width), F32),
            pltpu.VMEM((8, length), F32),
        ],
    )(*pieces, rows, matrices)


def matrix_kernel(cin_count, input_count, cout_count, *refs):
    pieces = refs[:cin_count]
    input_pieces = refs[cin_count : cin_count + input_count]
    rows_ref, out_ref, grads, inputs, inputs8, parts, parts8, bounds = refs[cin_count + input_count :]
    step = pl.program_id(0)
    _, length, _ = rows_ref.shape
    tokens = inputs.shape[0]
    seqs = tokens // length
    out_width = out_ref.shape[1]

    def table_of(first):
        table = rows_ref[pl.ds(first, 2)]
        return table.reshape(2 * length, 2 * length), reach_of(table, bounds[0:1, 0:1])

    def filter_sequence(slot, table, reach, b):
        filtered = lax.dot_general(
            grads[b * out_width : (b + 1) * out_width], table, (((1,), (1,)), ((), ())), preferred_element_type=F32
        )
        high, low = split(filtered)
        place = slice(b * length, (b + 1) * length)
        for k in range(2):
            columns = slice(k * length, (k + 1) * length)
            parts[2 * slot + k, :, place] = high[:, columns]
            parts8[2 * slot + k, :, place] = (low[:, columns] * (65536.0 / reach[k])).astype(F8)

    def filters_of(slot, table, reach):
        return [functools.partial(filter_sequence, slot, table, reach, b) for b in range(seqs)]

    def product(k, back):
        total = dot(parts[k], inputs[...]) + dot(parts8[k], inputs8[...]) * back
        out_ref[k] = total.astype(BF16)

    def products_of(slot, reach):
        backs = [(reach[k] / 65536.0) * (bounds[1:2, 0:1] / 256.0) for k in range(2)]
        return [functools.partial(product, 2 * slot + k, backs[k]) for k in range(2)]

    @pl.when(step == 0)
    def _():
        block = pieces[0].shape[0]
        for r, piece in enumerate(pieces):
            for b in range(seqs):
                rows = spot("cin", r, block, cin_count, b * out_width)
                part = piece[:, b * length : (b + 1) * length]
                grads[rows, :length] = part
                grads[rows, length:] = part
        gmax = functools.reduce(jnp.maximum, [largest(piece[...]) for piece in pieces])
        xmax = functools.reduce(jnp.maximum, [largest(piece[half]) for piece in input_pieces for half in range(piece.shape[0])])
        xmax = jnp.maximum(xmax, TINY)
        bounds[0:1, :] = jnp.broadcast_to(gmax, (1, length))
        bounds[1:2, :] = jnp.broadcast_to(xmax, (1, length))
        block = input_pieces[0].shape[1]
        for r, piece in enumerate(input_pieces):
            for half in range(piece.shape[0]):
                columns = spot("cout", 2 * r + half, block, cout_count)
                turned = piece[half].astype(F32).T
                inputs[:, columns] = turned.astype(BF16)
                inputs8[:, columns] = (turned * (256.0 / xmax)).astype(F8)
        for work in filters_of(0, *table_of(0)):
            work()

    now = table_of(GROUP * step)
    late = table_of(GROUP * step + 2)
    coming = table_of(lax.rem(GROUP * step + GROUP, rows_ref.shape[0]))
    interleave(filters_of(1, *late), products_of(0, now[1]))
    interleave(filters_of(0, *coming), products_of(1, late[1]))


def matrix_sums(pieces, input_pieces, rows, cout_count, shape):
    count, out_width, in_width = shape
    length = rows.shape[1]
    tokens = pieces[0].shape[1]
    seqs = tokens // length
    return call(
        functools.partial(matrix_kernel, len(pieces), len(input_pieces), cout_count),
        (3 * count * out_width * in_width * tokens, 2 * count * out_width * in_width),
        32,
        out_shape=jax.ShapeDtypeStruct(shape, BF16),
        grid=(count // GROUP,),
        in_specs=[whole(piece) for piece in (*pieces, *input_pieces)] + [whole(rows)],
        out_specs=pl.BlockSpec((GROUP, out_width, in_width), lambda i: (i, 0, 0)),
        scratch_shapes=[
            pltpu.VMEM((seqs * out_width, 2 * length), BF16),
            pltpu.VMEM((tokens, in_width), BF16),
            pltpu.VMEM((tokens, in_width), F8),
            pltpu.VMEM((GROUP, out_width, tokens), BF16),
            pltpu.VMEM((GROUP, out_width, tokens), F8),
            pltpu.VMEM((8, length), F32),
        ],
    )(*pieces, *input_pieces, rows)


def exchange(array, axis, count, flip):
    return lax.ppermute(array, axis, [(i, i ^ flip) for i in range(count)])


def shards(cin, cout, inputs, cotangent, matrices, filters):
    own, seq_count, length = inputs.shape
    tokens = seq_count * length
    flat_grads = cotangent.reshape(-1, tokens)
    if cin & (cin - 1) or flat_grads.shape[0] % 128:
        pieces = [lax.all_gather(flat_grads, "cin", axis=0, tiled=True)]
    else:
        pieces = [flat_grads] + [exchange(flat_grads, "cin", cin, flip) for flip in range(1, cin)]
    rows = make_tables(lax.optimization_barrier((filters, flat_grads))[0])
    flat_inputs = inputs.reshape(-1, tokens)
    if cout < 2 or cout & (cout - 1) or own % 128:
        input_pieces = [lax.all_gather(flat_inputs, "cout", axis=0, tiled=True)[None]]
        cout_count = 1
    else:
        both = jnp.concatenate([flat_inputs, exchange(flat_inputs, "cout", cout, 1)]).reshape(2, own, tokens)
        input_pieces = [both] + [exchange(both, "cout", cout, flip) for flip in range(2, cout, 2)]
        cout_count = cout

    blocks = back_sums(pieces, rows, matrices, cout).astype(F16)
    came = lax.all_to_all(blocks, "cout", 0, 0, tiled=True)
    matrix_grads = matrix_sums(pieces, input_pieces, rows, cout_count, matrices.shape)
    scales = jnp.exp2(came[:, own : own + 1].astype(F32) - 14.0)
    input_grads = jnp.sum(came[:, :own].astype(F32) * scales, axis=0).astype(BF16)
    return (matrix_grads, input_grads.reshape(own, seq_count, length))


def solution(mesh):
    placed = (
        P(("cin", "cout"), None, None),
        P(("cout", "cin"), None, None),
        P(None, "cout", "cin"),
        P(),
    )
    return jax.shard_map(
        functools.partial(shards, mesh.shape["cin"], mesh.shape["cout"]),
        mesh=mesh,
        in_specs=placed,
        out_specs=(P(None, "cout", "cin"), P(("cin", "cout"), None, None)),
        check_vma=False,
    )
```

```python
import functools
import itertools

import jax
import jax.numpy as jnp
from jax import lax
from jax.experimental import pallas as pl
from jax.experimental.pallas import tpu as pltpu
from jax.sharding import PartitionSpec as P

BF16 = jnp.bfloat16
F16 = jnp.float16
F32 = jnp.float32
F8 = jnp.float8_e4m3fn
MIB = 1024 * 1024
GROUP = 4
CHUNK = 256
TINY = 1e-30


def split(wide):
    high = wide.astype(BF16)
    return high, wide - high.astype(F32)


def dot(left, right):
    return jnp.dot(left, right, preferred_element_type=F32)


def call(body, cost, limit, **kwargs):
    flops, moved = cost
    return pl.pallas_call(
        body,
        compiler_params=pltpu.CompilerParams(vmem_limit_bytes=limit * MIB),
        cost_estimate=pl.CostEstimate(flops=flops, bytes_accessed=moved, transcendentals=0),
        **kwargs,
    )


def whole(array):
    return pl.BlockSpec(array.shape, lambda i: (0,) * len(array.shape))


def largest(array):
    return jnp.max(jnp.abs(array.astype(F32)), keepdims=True)


def spot(axis, flip, block, count, base=0):
    if count == 1:
        return slice(base, base + block)
    return pl.ds(pl.multiple_of(base + (lax.axis_index(axis) ^ flip) * block, block), block)


def reach_of(table, gmax):
    length = table.shape[1]
    sums = [jnp.sum(jnp.abs(table[k, 0:1, :length].astype(F32)), keepdims=True) for k in range(table.shape[0])]
    return [jnp.maximum(total * gmax, TINY) for total in sums]


def interleave(first, second):
    for one, other in itertools.zip_longest(first, second):
        for work in (one, other):
            if work is not None:
                work()


def chunks(width):
    size = min(width, CHUNK)
    return [slice(start, start + size) for start in range(0, width, size)]


def table_kernel(filters_ref, rows_ref):
    count, length = filters_ref.shape
    source = lax.broadcasted_iota(jnp.int32, (length, length), 0)
    token = lax.broadcasted_iota(jnp.int32, (length, length), 1)
    for k in range(count):
        spread = jnp.broadcast_to(filters_ref[k : k + 1, :], (length, length))
        shifted = pltpu.roll(spread, 0, 1, stride=1, stride_axis=0)
        high, low = split(jnp.where(token >= source, shifted, 0.0))
        rows_ref[k, :, :length] = high
        rows_ref[k, :, length:] = low.astype(BF16)


def make_tables(filters):
    count, length = filters.shape
    return call(
        table_kernel,
        (count * length * length * 4, count * length * length * 4),
        8,
        out_shape=jax.ShapeDtypeStruct((count, length, 2 * length), BF16),
    )(filters)


def back_kernel(cin_count, *refs):
    pieces = refs[:cin_count]
    rows_ref, matrix_ref, out, grads, parts, parts8, total, bounds = refs[cin_count:]
    step = pl.program_id(0)
    _, length, _ = rows_ref.shape
    out_width = matrix_ref.shape[1]
    seqs = grads.shape[1] // out_width
    tokens = seqs * length

    @pl.when(step == 0)
    def _():
        total[...] = jnp.zeros_like(total)
        block = pieces[0].shape[0]
        for b in range(seqs):
            for r, piece in enumerate(pieces):
                turned = piece[:, b * length : (b + 1) * length].astype(F32).T.astype(BF16)
                columns = spot("cin", r, block, cin_count, b * out_width)
                grads[:length, columns] = turned
                grads[length:, columns] = turned
        gmax = functools.reduce(jnp.maximum, [largest(piece[...]) for piece in pieces])
        bounds[...] = jnp.broadcast_to(gmax, bounds.shape)

    matrix = matrix_ref[...].reshape(GROUP * out_width, -1)
    peak = jnp.max(jnp.abs(matrix).reshape(-1, 16, matrix.shape[1]), axis=0)
    matrix_scale = (256.0 / jnp.maximum(largest(peak), TINY)).astype(BF16)
    matrix8 = (matrix * matrix_scale).astype(F8)
    table = rows_ref[pl.ds(GROUP * step, GROUP)]
    reach = functools.reduce(jnp.maximum, reach_of(table, bounds[0:1, 0:1]))
    table = table.reshape(GROUP * length, 2 * length)
    for b in range(seqs):
        high, low = split(dot(table, grads[:, b * out_width : (b + 1) * out_width]))
        low = (low * (65536.0 / reach)).astype(F8)
        for k in range(GROUP):
            source, columns = slice(k * length, (k + 1) * length), slice(k * out_width, (k + 1) * out_width)
            parts[b * length : (b + 1) * length, columns] = high[source]
            parts8[b * length : (b + 1) * length, columns] = low[source]
    back = (reach / 65536.0) / matrix_scale.astype(F32)
    total[...] += dot(parts[...], matrix) + dot(parts8[...], matrix8) * back

    @pl.when(step == pl.num_programs(0) - 1)
    def _():
        summed = total[...]
        exponent = jnp.floor(jnp.log2(jnp.maximum(largest(summed), TINY))) + 1.0
        summed = summed * jnp.exp2(14.0 - exponent)
        if out.shape[1] == tokens + 8:
            block = out.shape[2]
            for j in range(out.shape[0]):
                out[j, :tokens] = summed[:, j * block : (j + 1) * block]
                out[j, tokens:] = jnp.broadcast_to(exponent, (8, block))
        else:
            block = out.shape[1] - 8
            turned = summed.T
            for j in range(out.shape[0]):
                out[j, :block] = turned[j * block : (j + 1) * block]
                out[j, block:] = jnp.broadcast_to(exponent, (8, tokens))


def back_sums(pieces, rows, matrices, cout):
    count, out_width, in_width = matrices.shape
    length = rows.shape[1]
    tokens = pieces[0].shape[1]
    seqs = tokens // length
    own = in_width // cout
    shape = (tokens + 8, own) if own % 128 == 0 else (own + 8, tokens)
    out = jax.ShapeDtypeStruct((cout, *shape), F32)
    return call(
        functools.partial(back_kernel, len(pieces)),
        (4 * count * out_width * in_width * tokens, 2 * matrices.size),
        40,
        out_shape=out,
        grid=(count // GROUP,),
        in_specs=[whole(piece) for piece in pieces]
        + [whole(rows), pl.BlockSpec((GROUP, out_width, in_width), lambda i: (i, 0, 0))],
        out_specs=whole(out),
        scratch_shapes=[
            pltpu.VMEM((2 * length, seqs * out_width), BF16),
            pltpu.VMEM((tokens, GROUP * out_width), BF16),
            pltpu.VMEM((tokens, GROUP * out_width), F8),
            pltpu.VMEM((tokens, in_width), F32),
            pltpu.VMEM((8, length), F32),
        ],
    )(*pieces, rows, matrices)


def matrix_kernel(cin_count, input_count, cout_count, *refs):
    pieces = refs[:cin_count]
    input_pieces = refs[cin_count : cin_count + input_count]
    rows_ref, out_ref, grads, inputs, inputs8, parts, parts8, bounds = refs[cin_count + input_count :]
    step = pl.program_id(0)
    _, length, _ = rows_ref.shape
    tokens = inputs.shape[0]
    seqs = tokens // length
    out_width = out_ref.shape[1]

    def table_of(first):
        table = rows_ref[pl.ds(first, 2)]
        return table.reshape(2 * length, 2 * length), reach_of(table, bounds[0:1, 0:1])

    def filter_sequence(slot, table, reach, b):
        filtered = lax.dot_general(
            grads[b * out_width : (b + 1) * out_width], table, (((1,), (1,)), ((), ())), preferred_element_type=F32
        )
        high, low = split(filtered)
        place = slice(b * length, (b + 1) * length)
        for k in range(2):
            columns = slice(k * length, (k + 1) * length)
            parts[2 * slot + k, :, place] = high[:, columns]
            parts8[2 * slot + k, :, place] = (low[:, columns] * (65536.0 / reach[k])).astype(F8)

    def filters_of(slot, table, reach):
        return [functools.partial(filter_sequence, slot, table, reach, b) for b in range(seqs)]

    def product(k, back, columns):
        total = dot(parts[k], inputs[:, columns]) + dot(parts8[k], inputs8[:, columns]) * back
        out_ref[k, :, columns] = total.astype(BF16)

    def products_of(slot, reach):
        backs = [(reach[k] / 65536.0) * (bounds[1:2, 0:1] / 256.0) for k in range(2)]
        return [
            functools.partial(product, 2 * slot + k, backs[k], columns)
            for k in range(2)
            for columns in chunks(inputs.shape[1])
        ]

    @pl.when(step == 0)
    def _():
        block = pieces[0].shape[0]
        for r, piece in enumerate(pieces):
            for b in range(seqs):
                rows = spot("cin", r, block, cin_count, b * out_width)
                part = piece[:, b * length : (b + 1) * length]
                grads[rows, :length] = part
                grads[rows, length:] = part
        gmax = functools.reduce(jnp.maximum, [largest(piece[...]) for piece in pieces])
        xmax = functools.reduce(jnp.maximum, [largest(piece[half]) for piece in input_pieces for half in range(piece.shape[0])])
        xmax = jnp.maximum(xmax, TINY)
        bounds[0:1, :] = jnp.broadcast_to(gmax, (1, length))
        bounds[1:2, :] = jnp.broadcast_to(xmax, (1, length))
        block = input_pieces[0].shape[1]
        for r, piece in enumerate(input_pieces):
            for half in range(piece.shape[0]):
                columns = spot("cout", 2 * r + half, block, cout_count)
                turned = piece[half].astype(F32).T
                inputs[:, columns] = turned.astype(BF16)
                inputs8[:, columns] = (turned * (256.0 / xmax)).astype(F8)
        interleave(filters_of(0, *table_of(0)), [])

    now = table_of(GROUP * step)
    late = table_of(GROUP * step + 2)
    coming = table_of(lax.rem(GROUP * step + GROUP, rows_ref.shape[0]))
    interleave(products_of(0, now[1]), filters_of(1, *late))
    interleave(products_of(1, late[1]), filters_of(0, *coming))


def matrix_sums(pieces, input_pieces, rows, cout_count, shape):
    count, out_width, in_width = shape
    length = rows.shape[1]
    tokens = pieces[0].shape[1]
    seqs = tokens // length
    return call(
        functools.partial(matrix_kernel, len(pieces), len(input_pieces), cout_count),
        (3 * count * out_width * in_width * tokens, 2 * count * out_width * in_width),
        32,
        out_shape=jax.ShapeDtypeStruct(shape, BF16),
        grid=(count // GROUP,),
        in_specs=[whole(piece) for piece in (*pieces, *input_pieces)] + [whole(rows)],
        out_specs=pl.BlockSpec((GROUP, out_width, in_width), lambda i: (i, 0, 0)),
        scratch_shapes=[
            pltpu.VMEM((seqs * out_width, 2 * length), BF16),
            pltpu.VMEM((tokens, in_width), BF16),
            pltpu.VMEM((tokens, in_width), F8),
            pltpu.VMEM((GROUP, out_width, tokens), BF16),
            pltpu.VMEM((GROUP, out_width, tokens), F8),
            pltpu.VMEM((8, length), F32),
        ],
    )(*pieces, *input_pieces, rows)


def exchange(array, axis, count, flip):
    return lax.ppermute(array, axis, [(i, i ^ flip) for i in range(count)])


def shards(cin, cout, inputs, cotangent, matrices, filters):
    own, seq_count, length = inputs.shape
    tokens = seq_count * length
    flat_grads = cotangent.reshape(-1, tokens)
    if cin & (cin - 1) or flat_grads.shape[0] % 128:
        pieces = [lax.all_gather(flat_grads, "cin", axis=0, tiled=True)]
    else:
        pieces = [flat_grads] + [exchange(flat_grads, "cin", cin, flip) for flip in range(1, cin)]
    rows = make_tables(lax.optimization_barrier((filters, flat_grads))[0])
    flat_inputs = inputs.reshape(-1, tokens)
    if cout < 2 or cout & (cout - 1) or own % 128:
        input_pieces = [lax.all_gather(flat_inputs, "cout", axis=0, tiled=True)[None]]
        cout_count = 1
    else:
        both = jnp.concatenate([flat_inputs, exchange(flat_inputs, "cout", cout, 1)]).reshape(2, own, tokens)
        input_pieces = [both] + [exchange(both, "cout", cout, flip) for flip in range(2, cout, 2)]
        cout_count = cout

    blocks = back_sums(pieces, rows, matrices, cout).astype(F16)
    came = lax.all_to_all(blocks, "cout", 0, 0, tiled=True)
    matrix_grads = matrix_sums(pieces, input_pieces, rows, cout_count, matrices.shape)
    rows = came.shape[1] - 8
    scales = jnp.exp2(came[:, rows : rows + 1].astype(F32) - 14.0)
    input_grads = jnp.sum(came[:, :rows].astype(F32) * scales, axis=0).astype(BF16)
    if rows == tokens:
        input_grads = input_grads.reshape(seq_count, length, own).transpose(2, 0, 1)
    return (matrix_grads, input_grads.reshape(own, seq_count, length))


def solution(mesh):
    placed = (
        P(("cin", "cout"), None, None),
        P(("cout", "cin"), None, None),
        P(None, "cout", "cin"),
        P(),
    )
    return jax.shard_map(
        functools.partial(shards, mesh.shape["cin"], mesh.shape["cout"]),
        mesh=mesh,
        in_specs=placed,
        out_specs=(P(None, "cout", "cin"), P(("cin", "cout"), None, None)),
        check_vma=False,
    )
```

```python
import functools
import itertools

import jax
import jax.numpy as jnp
from jax import lax
from jax.experimental import pallas as pl
from jax.experimental.pallas import tpu as pltpu
from jax.sharding import PartitionSpec as P

BF16 = jnp.bfloat16
F16 = jnp.float16
F32 = jnp.float32
F8 = jnp.float8_e4m3fn
MIB = 1024 * 1024
GROUP = 4
CHUNK = 256
TINY = 1e-30


def split(wide):
    high = wide.astype(BF16)
    return high, wide - high.astype(F32)


def dot(left, right):
    return jnp.dot(left, right, preferred_element_type=F32)


def call(body, cost, limit, **kwargs):
    flops, moved = cost
    return pl.pallas_call(
        body,
        compiler_params=pltpu.CompilerParams(vmem_limit_bytes=limit * MIB),
        cost_estimate=pl.CostEstimate(flops=flops, bytes_accessed=moved, transcendentals=0),
        **kwargs,
    )


def whole(array):
    return pl.BlockSpec(array.shape, lambda i: (0,) * len(array.shape))


def largest(array):
    return jnp.max(jnp.abs(array.astype(F32)), keepdims=True)


def spot(axis, flip, block, count, base=0):
    if count == 1:
        return slice(base, base + block)
    return pl.ds(pl.multiple_of(base + (lax.axis_index(axis) ^ flip) * block, block), block)


def reach_of(table, gmax):
    length = table.shape[1]
    sums = [jnp.sum(jnp.abs(table[k, 0:1, :length].astype(F32)), keepdims=True) for k in range(table.shape[0])]
    return [jnp.maximum(total * gmax, TINY) for total in sums]


def interleave(first, second):
    for one, other in itertools.zip_longest(first, second):
        for work in (one, other):
            if work is not None:
                work()


def chunks(width):
    size = min(width, CHUNK)
    return [slice(start, start + size) for start in range(0, width, size)]


def table_kernel(filters_ref, rows_ref):
    count, length = filters_ref.shape
    source = lax.broadcasted_iota(jnp.int32, (length, length), 0)
    token = lax.broadcasted_iota(jnp.int32, (length, length), 1)
    for k in range(count):
        spread = jnp.broadcast_to(filters_ref[k : k + 1, :], (length, length))
        shifted = pltpu.roll(spread, 0, 1, stride=1, stride_axis=0)
        high, low = split(jnp.where(token >= source, shifted, 0.0))
        rows_ref[k, :, :length] = high
        rows_ref[k, :, length:] = low.astype(BF16)


def make_tables(filters):
    count, length = filters.shape
    return call(
        table_kernel,
        (count * length * length * 4, count * length * length * 4),
        8,
        out_shape=jax.ShapeDtypeStruct((count, length, 2 * length), BF16),
    )(filters)


def back_kernel(cin_count, *refs):
    pieces = refs[:cin_count]
    rows_ref, matrix_ref, out, grads, parts, parts8, total, bounds = refs[cin_count:]
    step = pl.program_id(0)
    _, length, _ = rows_ref.shape
    out_width = matrix_ref.shape[1]
    seqs = grads.shape[1] // out_width
    tokens = seqs * length

    @pl.when(step == 0)
    def _():
        total[...] = jnp.zeros_like(total)
        block = pieces[0].shape[0]
        for b in range(seqs):
            for r, piece in enumerate(pieces):
                turned = piece[:, b * length : (b + 1) * length].astype(F32).T.astype(BF16)
                columns = spot("cin", r, block, cin_count, b * out_width)
                grads[:length, columns] = turned
                grads[length:, columns] = turned
        gmax = functools.reduce(jnp.maximum, [largest(piece[...]) for piece in pieces])
        bounds[...] = jnp.broadcast_to(gmax, bounds.shape)

    matrix = matrix_ref[...].reshape(GROUP * out_width, -1)
    peak = jnp.max(jnp.abs(matrix).reshape(-1, 16, matrix.shape[1]), axis=0)
    matrix_scale = (256.0 / jnp.maximum(largest(peak), TINY)).astype(BF16)
    matrix8 = (matrix * matrix_scale).astype(F8)
    table = rows_ref[pl.ds(GROUP * step, GROUP)]
    reach = functools.reduce(jnp.maximum, reach_of(table, bounds[0:1, 0:1]))
    table = table.reshape(GROUP * length, 2 * length)
    for b in range(seqs):
        high, low = split(dot(table, grads[:, b * out_width : (b + 1) * out_width]))
        low = (low * (65536.0 / reach)).astype(F8)
        for k in range(GROUP):
            source, columns = slice(k * length, (k + 1) * length), slice(k * out_width, (k + 1) * out_width)
            parts[b * length : (b + 1) * length, columns] = high[source]
            parts8[b * length : (b + 1) * length, columns] = low[source]
    back = (reach / 65536.0) / matrix_scale.astype(F32)
    total[...] += dot(parts[...], matrix) + dot(parts8[...], matrix8) * back

    @pl.when(step == pl.num_programs(0) - 1)
    def _():
        summed = total[...]
        exponent = jnp.floor(jnp.log2(jnp.maximum(largest(summed), TINY))) + 1.0
        summed = summed * jnp.exp2(14.0 - exponent)
        if out.shape[1] == tokens + 8:
            block = out.shape[2]
            for j in range(out.shape[0]):
                out[j, :tokens] = summed[:, j * block : (j + 1) * block]
                out[j, tokens:] = jnp.broadcast_to(exponent, (8, block))
        else:
            block = out.shape[1] - 8
            turned = summed.T
            for j in range(out.shape[0]):
                out[j, :block] = turned[j * block : (j + 1) * block]
                out[j, block:] = jnp.broadcast_to(exponent, (8, tokens))


def back_sums(pieces, rows, matrices, cout):
    count, out_width, in_width = matrices.shape
    length = rows.shape[1]
    tokens = pieces[0].shape[1]
    seqs = tokens // length
    own = in_width // cout
    shape = (tokens + 8, own) if own % 128 == 0 else (own + 8, tokens)
    out = jax.ShapeDtypeStruct((cout, *shape), F32)
    return call(
        functools.partial(back_kernel, len(pieces)),
        (4 * count * out_width * in_width * tokens, 2 * matrices.size),
        40,
        out_shape=out,
        grid=(count // GROUP,),
        in_specs=[whole(piece) for piece in pieces]
        + [whole(rows), pl.BlockSpec((GROUP, out_width, in_width), lambda i: (i, 0, 0))],
        out_specs=whole(out),
        scratch_shapes=[
            pltpu.VMEM((2 * length, seqs * out_width), BF16),
            pltpu.VMEM((tokens, GROUP * out_width), BF16),
            pltpu.VMEM((tokens, GROUP * out_width), F8),
            pltpu.VMEM((tokens, in_width), F32),
            pltpu.VMEM((8, length), F32),
        ],
    )(*pieces, rows, matrices)


def matrix_kernel(cin_count, input_count, cout_count, *refs):
    pieces = refs[:cin_count]
    input_pieces = refs[cin_count : cin_count + input_count]
    rows_ref, out_ref, grads, inputs, inputs8, parts, parts8, bounds = refs[cin_count + input_count :]
    step = pl.program_id(0)
    _, length, _ = rows_ref.shape
    tokens = inputs.shape[0]
    seqs = tokens // length
    out_width = out_ref.shape[1]

    def table_of(first):
        table = rows_ref[pl.ds(first, 2)]
        return table.reshape(2 * length, 2 * length), reach_of(table, bounds[0:1, 0:1])

    def filter_sequence(slot, table, reach, b):
        filtered = lax.dot_general(
            grads[b * out_width : (b + 1) * out_width], table, (((1,), (1,)), ((), ())), preferred_element_type=F32
        )
        high, low = split(filtered)
        place = slice(b * length, (b + 1) * length)
        for k in range(2):
            columns = slice(k * length, (k + 1) * length)
            parts[2 * slot + k, :, place] = high[:, columns]
            parts8[2 * slot + k, :, place] = (low[:, columns] * (65536.0 / reach[k])).astype(F8)

    def filters_of(slot, table, reach):
        return [functools.partial(filter_sequence, slot, table, reach, b) for b in range(seqs)]

    def product(k, back, columns):
        total = dot(parts[k], inputs[:, columns]) + dot(parts8[k], inputs8[:, columns]) * back
        out_ref[k, :, columns] = total.astype(BF16)

    def products_of(slot, reach):
        backs = [(reach[k] / 65536.0) * (bounds[1:2, 0:1] / 256.0) for k in range(2)]
        return [
            functools.partial(product, 2 * slot + k, backs[k], columns)
            for k in range(2)
            for columns in chunks(inputs.shape[1])
        ]

    @pl.when(step == 0)
    def _():
        block = pieces[0].shape[0]
        for r, piece in enumerate(pieces):
            for b in range(seqs):
                rows = spot("cin", r, block, cin_count, b * out_width)
                part = piece[:, b * length : (b + 1) * length]
                grads[rows, :length] = part
                grads[rows, length:] = part
        gmax = functools.reduce(jnp.maximum, [largest(piece[...]) for piece in pieces])
        xmax = functools.reduce(jnp.maximum, [largest(piece[half]) for piece in input_pieces for half in range(piece.shape[0])])
        xmax = jnp.maximum(xmax, TINY)
        bounds[0:1, :] = jnp.broadcast_to(gmax, (1, length))
        bounds[1:2, :] = jnp.broadcast_to(xmax, (1, length))
        block = input_pieces[0].shape[2]
        for r, piece in enumerate(input_pieces):
            for half in range(piece.shape[0]):
                columns = spot("cout", 2 * r + half, block, cout_count)
                inputs[:, columns] = piece[half]
                inputs8[:, columns] = (piece[half].astype(F32) * (256.0 / xmax)).astype(F8)
        interleave(filters_of(0, *table_of(0)), [])

    now = table_of(GROUP * step)
    late = table_of(GROUP * step + 2)
    coming = table_of(lax.rem(GROUP * step + GROUP, rows_ref.shape[0]))
    interleave(products_of(0, now[1]), filters_of(1, *late))
    interleave(products_of(1, late[1]), filters_of(0, *coming))


def matrix_sums(pieces, input_pieces, rows, cout_count, shape):
    count, out_width, in_width = shape
    length = rows.shape[1]
    tokens = pieces[0].shape[1]
    seqs = tokens // length
    return call(
        functools.partial(matrix_kernel, len(pieces), len(input_pieces), cout_count),
        (3 * count * out_width * in_width * tokens, 2 * count * out_width * in_width),
        32,
        out_shape=jax.ShapeDtypeStruct(shape, BF16),
        grid=(count // GROUP,),
        in_specs=[whole(piece) for piece in (*pieces, *input_pieces)] + [whole(rows)],
        out_specs=pl.BlockSpec((GROUP, out_width, in_width), lambda i: (i, 0, 0)),
        scratch_shapes=[
            pltpu.VMEM((seqs * out_width, 2 * length), BF16),
            pltpu.VMEM((tokens, in_width), BF16),
            pltpu.VMEM((tokens, in_width), F8),
            pltpu.VMEM((GROUP, out_width, tokens), BF16),
            pltpu.VMEM((GROUP, out_width, tokens), F8),
            pltpu.VMEM((8, length), F32),
        ],
    )(*pieces, *input_pieces, rows)


def exchange(array, axis, count, flip):
    return lax.ppermute(array, axis, [(i, i ^ flip) for i in range(count)])


def shards(cin, cout, inputs, cotangent, matrices, filters):
    own, seq_count, length = inputs.shape
    tokens = seq_count * length
    flat_grads = cotangent.reshape(-1, tokens)
    if cin & (cin - 1) or flat_grads.shape[0] % 128:
        pieces = [lax.all_gather(flat_grads, "cin", axis=0, tiled=True)]
    else:
        pieces = [flat_grads] + [exchange(flat_grads, "cin", cin, flip) for flip in range(1, cin)]
    rows = make_tables(lax.optimization_barrier((filters, flat_grads))[0])
    turned = inputs.transpose(1, 2, 0).reshape(tokens, own)
    if cout < 2 or cout & (cout - 1) or own % 128:
        input_pieces = [lax.all_gather(turned, "cout", axis=1, tiled=True)[None]]
        cout_count = 1
    else:
        both = jnp.concatenate([turned, exchange(turned, "cout", cout, 1)]).reshape(2, tokens, own)
        input_pieces = [both] + [exchange(both, "cout", cout, flip) for flip in range(2, cout, 2)]
        cout_count = cout

    blocks = back_sums(pieces, rows, matrices, cout).astype(F16)
    came = lax.all_to_all(blocks, "cout", 0, 0, tiled=True)
    matrix_grads = matrix_sums(pieces, input_pieces, rows, cout_count, matrices.shape)
    rows = came.shape[1] - 8
    scales = jnp.exp2(came[:, rows : rows + 1].astype(F32) - 14.0)
    input_grads = jnp.sum(came[:, :rows].astype(F32) * scales, axis=0).astype(BF16)
    if rows == tokens:
        input_grads = input_grads.reshape(seq_count, length, own).transpose(2, 0, 1)
    return (matrix_grads, input_grads.reshape(own, seq_count, length))


def solution(mesh):
    placed = (
        P(("cin", "cout"), None, None),
        P(("cout", "cin"), None, None),
        P(None, "cout", "cin"),
        P(),
    )
    return jax.shard_map(
        functools.partial(shards, mesh.shape["cin"], mesh.shape["cout"]),
        mesh=mesh,
        in_specs=placed,
        out_specs=(P(None, "cout", "cin"), P(("cin", "cout"), None, None)),
        check_vma=False,
    )
```

```python
import functools
import itertools

import jax
import jax.numpy as jnp
from jax import lax
from jax.experimental import pallas as pl
from jax.experimental.pallas import tpu as pltpu
from jax.sharding import PartitionSpec as P

BF16 = jnp.bfloat16
F16 = jnp.float16
F32 = jnp.float32
F8 = jnp.float8_e4m3fn
MIB = 1024 * 1024
GROUP = 4
CHUNK = 256
TINY = 1e-30


def split(wide):
    high = wide.astype(BF16)
    return high, wide - high.astype(F32)


def dot(left, right):
    return jnp.dot(left, right, preferred_element_type=F32)


def call(body, cost, limit, **kwargs):
    flops, moved = cost
    return pl.pallas_call(
        body,
        compiler_params=pltpu.CompilerParams(vmem_limit_bytes=limit * MIB),
        cost_estimate=pl.CostEstimate(flops=flops, bytes_accessed=moved, transcendentals=0),
        **kwargs,
    )


def whole(array):
    return pl.BlockSpec(array.shape, lambda i: (0,) * len(array.shape))


def largest(array):
    return jnp.max(jnp.abs(array.astype(F32)), keepdims=True)


def spot(axis, flip, block, count, base=0):
    if count == 1:
        return slice(base, base + block)
    return pl.ds(pl.multiple_of(base + (lax.axis_index(axis) ^ flip) * block, block), block)


def reach_of(table, gmax):
    length = table.shape[1]
    sums = [jnp.sum(jnp.abs(table[k, 0:1, :length].astype(F32)), keepdims=True) for k in range(table.shape[0])]
    return [jnp.maximum(total * gmax, TINY) for total in sums]


def interleave(first, second):
    for one, other in itertools.zip_longest(first, second):
        for work in (one, other):
            if work is not None:
                work()


def chunks(width):
    size = min(width, CHUNK)
    return [slice(start, start + size) for start in range(0, width, size)]


def table_kernel(filters_ref, rows_ref):
    count, length = filters_ref.shape
    source = lax.broadcasted_iota(jnp.int32, (length, length), 0)
    token = lax.broadcasted_iota(jnp.int32, (length, length), 1)
    for k in range(count):
        spread = jnp.broadcast_to(filters_ref[k : k + 1, :], (length, length))
        shifted = pltpu.roll(spread, 0, 1, stride=1, stride_axis=0)
        high, low = split(jnp.where(token >= source, shifted, 0.0))
        rows_ref[k, :, :length] = high
        rows_ref[k, :, length:] = low.astype(BF16)


def make_tables(filters):
    count, length = filters.shape
    return call(
        table_kernel,
        (count * length * length * 4, count * length * length * 4),
        8,
        out_shape=jax.ShapeDtypeStruct((count, length, 2 * length), BF16),
    )(filters)


def back_kernel(cin_count, *refs):
    pieces = refs[:cin_count]
    rows_ref, matrix_ref, out, grads, parts, parts8, total, bounds, matrix8 = refs[cin_count:]
    step = pl.program_id(0)
    _, length, _ = rows_ref.shape
    out_width = matrix_ref.shape[1]
    seqs = grads.shape[1] // out_width
    tokens = seqs * length

    @pl.when(step == 0)
    def _():
        total[...] = jnp.zeros_like(total)
        block = pieces[0].shape[0]
        for b in range(seqs):
            for r, piece in enumerate(pieces):
                turned = piece[:, b * length : (b + 1) * length].astype(F32).T.astype(BF16)
                columns = spot("cin", r, block, cin_count, b * out_width)
                grads[:length, columns] = turned
                grads[length:, columns] = turned
        gmax = functools.reduce(jnp.maximum, [largest(piece[...]) for piece in pieces])
        bounds[...] = jnp.broadcast_to(gmax, bounds.shape)

    table = rows_ref[pl.ds(GROUP * step, GROUP)]
    reach = functools.reduce(jnp.maximum, reach_of(table, bounds[0:1, 0:1]))
    table = table.reshape(GROUP * length, 2 * length)
    for b in range(seqs):
        high, low = split(dot(table, grads[:, b * out_width : (b + 1) * out_width]))
        low = (low * (65536.0 / reach)).astype(F8)
        for k in range(GROUP):
            source, columns = slice(k * length, (k + 1) * length), slice(k * out_width, (k + 1) * out_width)
            parts[b * length : (b + 1) * length, columns] = high[source]
            parts8[b * length : (b + 1) * length, columns] = low[source]
        if b == 0:
            peak = jnp.max(jnp.abs(matrix_ref[...]).reshape(-1, 16, matrix_ref.shape[2]), axis=0)
            matrix_scale = (256.0 / jnp.maximum(largest(peak), TINY)).astype(BF16)
        for k in range(b, GROUP, seqs):
            matrix8[k * out_width : (k + 1) * out_width] = (matrix_ref[k] * matrix_scale).astype(F8)
    matrix = matrix_ref[...].reshape(GROUP * out_width, -1)
    back = (reach / 65536.0) / matrix_scale.astype(F32)
    total[...] += dot(parts[...], matrix) + dot(parts8[...], matrix8[...]) * back

    @pl.when(step == pl.num_programs(0) - 1)
    def _():
        summed = total[...]
        exponent = jnp.floor(jnp.log2(jnp.maximum(largest(summed), TINY))) + 1.0
        summed = summed * jnp.exp2(14.0 - exponent)
        if out.shape[1] == tokens + 8:
            block = out.shape[2]
            for j in range(out.shape[0]):
                out[j, :tokens] = summed[:, j * block : (j + 1) * block]
                out[j, tokens:] = jnp.broadcast_to(exponent, (8, block))
        else:
            block = out.shape[1] - 8
            turned = summed.T
            for j in range(out.shape[0]):
                out[j, :block] = turned[j * block : (j + 1) * block]
                out[j, block:] = jnp.broadcast_to(exponent, (8, tokens))


def back_sums(pieces, rows, matrices, cout):
    count, out_width, in_width = matrices.shape
    length = rows.shape[1]
    tokens = pieces[0].shape[1]
    seqs = tokens // length
    own = in_width // cout
    shape = (tokens + 8, own) if own % 128 == 0 else (own + 8, tokens)
    out = jax.ShapeDtypeStruct((cout, *shape), F32)
    return call(
        functools.partial(back_kernel, len(pieces)),
        (4 * count * out_width * in_width * tokens, 2 * matrices.size),
        40,
        out_shape=out,
        grid=(count // GROUP,),
        in_specs=[whole(piece) for piece in pieces]
        + [whole(rows), pl.BlockSpec((GROUP, out_width, in_width), lambda i: (i, 0, 0))],
        out_specs=whole(out),
        scratch_shapes=[
            pltpu.VMEM((2 * length, seqs * out_width), BF16),
            pltpu.VMEM((tokens, GROUP * out_width), BF16),
            pltpu.VMEM((tokens, GROUP * out_width), F8),
            pltpu.VMEM((tokens, in_width), F32),
            pltpu.VMEM((8, length), F32),
            pltpu.VMEM((GROUP * out_width, in_width), F8),
        ],
    )(*pieces, rows, matrices)


def matrix_kernel(cin_count, input_count, cout_count, *refs):
    pieces = refs[:cin_count]
    input_pieces = refs[cin_count : cin_count + input_count]
    rows_ref, out_ref, grads, inputs, inputs8, parts, parts8, bounds = refs[cin_count + input_count :]
    step = pl.program_id(0)
    _, length, _ = rows_ref.shape
    tokens = inputs.shape[0]
    seqs = tokens // length
    out_width = out_ref.shape[1]

    def table_of(first):
        table = rows_ref[pl.ds(first, 2)]
        return table.reshape(2 * length, 2 * length), reach_of(table, bounds[0:1, 0:1])

    def filter_sequence(slot, table, reach, b):
        filtered = lax.dot_general(
            grads[b * out_width : (b + 1) * out_width], table, (((1,), (1,)), ((), ())), preferred_element_type=F32
        )
        high, low = split(filtered)
        place = slice(b * length, (b + 1) * length)
        for k in range(2):
            columns = slice(k * length, (k + 1) * length)
            parts[2 * slot + k, :, place] = high[:, columns]
            parts8[2 * slot + k, :, place] = (low[:, columns] * (65536.0 / reach[k])).astype(F8)

    def filters_of(slot, table, reach):
        return [functools.partial(filter_sequence, slot, table, reach, b) for b in range(seqs)]

    def product(k, back, columns):
        total = dot(parts[k], inputs[:, columns]) + dot(parts8[k], inputs8[:, columns]) * back
        out_ref[k, :, columns] = total.astype(BF16)

    def products_of(slot, reach):
        backs = [(reach[k] / 65536.0) * (bounds[1:2, 0:1] / 256.0) for k in range(2)]
        return [
            functools.partial(product, 2 * slot + k, backs[k], columns)
            for k in range(2)
            for columns in chunks(inputs.shape[1])
        ]

    @pl.when(step == 0)
    def _():
        block = pieces[0].shape[0]
        for r, piece in enumerate(pieces):
            for b in range(seqs):
                rows = spot("cin", r, block, cin_count, b * out_width)
                part = piece[:, b * length : (b + 1) * length]
                grads[rows, :length] = part
                grads[rows, length:] = part
        gmax = functools.reduce(jnp.maximum, [largest(piece[...]) for piece in pieces])
        xmax = functools.reduce(jnp.maximum, [largest(piece[half]) for piece in input_pieces for half in range(piece.shape[0])])
        xmax = jnp.maximum(xmax, TINY)
        bounds[0:1, :] = jnp.broadcast_to(gmax, (1, length))
        bounds[1:2, :] = jnp.broadcast_to(xmax, (1, length))
        block = input_pieces[0].shape[1]
        for r, piece in enumerate(input_pieces):
            for half in range(piece.shape[0]):
                columns = spot("cout", 2 * r + half, block, cout_count)
                turned = piece[half].astype(F32).T
                inputs[:, columns] = turned.astype(BF16)
                inputs8[:, columns] = (turned * (256.0 / xmax)).astype(F8)
        interleave(filters_of(0, *table_of(0)), [])

    now = table_of(GROUP * step)
    late = table_of(GROUP * step + 2)
    coming = table_of(lax.rem(GROUP * step + GROUP, rows_ref.shape[0]))
    interleave(products_of(0, now[1]), filters_of(1, *late))
    interleave(products_of(1, late[1]), filters_of(0, *coming))


def matrix_sums(pieces, input_pieces, rows, cout_count, shape):
    count, out_width, in_width = shape
    length = rows.shape[1]
    tokens = pieces[0].shape[1]
    seqs = tokens // length
    return call(
        functools.partial(matrix_kernel, len(pieces), len(input_pieces), cout_count),
        (3 * count * out_width * in_width * tokens, 2 * count * out_width * in_width),
        32,
        out_shape=jax.ShapeDtypeStruct(shape, BF16),
        grid=(count // GROUP,),
        in_specs=[whole(piece) for piece in (*pieces, *input_pieces)] + [whole(rows)],
        out_specs=pl.BlockSpec((GROUP, out_width, in_width), lambda i: (i, 0, 0)),
        scratch_shapes=[
            pltpu.VMEM((seqs * out_width, 2 * length), BF16),
            pltpu.VMEM((tokens, in_width), BF16),
            pltpu.VMEM((tokens, in_width), F8),
            pltpu.VMEM((GROUP, out_width, tokens), BF16),
            pltpu.VMEM((GROUP, out_width, tokens), F8),
            pltpu.VMEM((8, length), F32),
        ],
    )(*pieces, *input_pieces, rows)


def exchange(array, axis, count, flip):
    return lax.ppermute(array, axis, [(i, i ^ flip) for i in range(count)])


def shards(cin, cout, inputs, cotangent, matrices, filters):
    own, seq_count, length = inputs.shape
    tokens = seq_count * length
    flat_grads = cotangent.reshape(-1, tokens)
    if cin & (cin - 1) or flat_grads.shape[0] % 128:
        pieces = [lax.all_gather(flat_grads, "cin", axis=0, tiled=True)]
    else:
        pieces = [flat_grads] + [exchange(flat_grads, "cin", cin, flip) for flip in range(1, cin)]
    rows = make_tables(lax.optimization_barrier((filters, flat_grads))[0])
    flat_inputs = inputs.reshape(-1, tokens)
    if cout < 2 or cout & (cout - 1) or own % 128:
        input_pieces = [lax.all_gather(flat_inputs, "cout", axis=0, tiled=True)[None]]
        cout_count = 1
    else:
        both = jnp.concatenate([flat_inputs, exchange(flat_inputs, "cout", cout, 1)]).reshape(2, own, tokens)
        input_pieces = [both] + [exchange(both, "cout", cout, flip) for flip in range(2, cout, 2)]
        cout_count = cout

    blocks = back_sums(pieces, rows, matrices, cout).astype(F16)
    came = lax.all_to_all(blocks, "cout", 0, 0, tiled=True)
    matrix_grads = matrix_sums(pieces, input_pieces, rows, cout_count, matrices.shape)
    rows = came.shape[1] - 8
    scales = jnp.exp2(came[:, rows : rows + 1].astype(F32) - 14.0)
    input_grads = jnp.sum(came[:, :rows].astype(F32) * scales, axis=0).astype(BF16)
    if rows == tokens:
        input_grads = input_grads.reshape(seq_count, length, own).transpose(2, 0, 1)
    return (matrix_grads, input_grads.reshape(own, seq_count, length))


def solution(mesh):
    placed = (
        P(("cin", "cout"), None, None),
        P(("cout", "cin"), None, None),
        P(None, "cout", "cin"),
        P(),
    )
    return jax.shard_map(
        functools.partial(shards, mesh.shape["cin"], mesh.shape["cout"]),
        mesh=mesh,
        in_specs=placed,
        out_specs=(P(None, "cout", "cin"), P(("cin", "cout"), None, None)),
        check_vma=False,
    )
```

```python
import functools
import itertools

import jax
import jax.numpy as jnp
from jax import lax
from jax.experimental import pallas as pl
from jax.experimental.pallas import tpu as pltpu
from jax.sharding import PartitionSpec as P

BF16 = jnp.bfloat16
F16 = jnp.float16
F32 = jnp.float32
F8 = jnp.float8_e4m3fn
MIB = 1024 * 1024
GROUP = 4
CHUNK = 256
TINY = 1e-30


def split(wide):
    high = wide.astype(BF16)
    return high, wide - high.astype(F32)


def dot(left, right):
    return jnp.dot(left, right, preferred_element_type=F32)


def call(body, cost, limit, **kwargs):
    flops, moved = cost
    return pl.pallas_call(
        body,
        compiler_params=pltpu.CompilerParams(vmem_limit_bytes=limit * MIB),
        cost_estimate=pl.CostEstimate(flops=flops, bytes_accessed=moved, transcendentals=0),
        **kwargs,
    )


def whole(array):
    return pl.BlockSpec(array.shape, lambda i: (0,) * len(array.shape))


def largest(array):
    return jnp.max(jnp.abs(array.astype(F32)), keepdims=True)


def spot(axis, flip, block, count, base=0):
    if count == 1:
        return slice(base, base + block)
    return pl.ds(pl.multiple_of(base + (lax.axis_index(axis) ^ flip) * block, block), block)


def reach_of(table, gmax):
    length = table.shape[1]
    sums = [jnp.sum(jnp.abs(table[k, 0:1, :length].astype(F32)), keepdims=True) for k in range(table.shape[0])]
    return [jnp.maximum(total * gmax, TINY) for total in sums]


def interleave(first, second):
    for one, other in itertools.zip_longest(first, second):
        for work in (one, other):
            if work is not None:
                work()


def chunks(width):
    size = min(width, CHUNK)
    return [slice(start, start + size) for start in range(0, width, size)]


def table_kernel(filters_ref, rows_ref):
    count, length = filters_ref.shape
    source = lax.broadcasted_iota(jnp.int32, (length, length), 0)
    token = lax.broadcasted_iota(jnp.int32, (length, length), 1)
    for k in range(count):
        spread = jnp.broadcast_to(filters_ref[k : k + 1, :], (length, length))
        shifted = pltpu.roll(spread, 0, 1, stride=1, stride_axis=0)
        high, low = split(jnp.where(token >= source, shifted, 0.0))
        rows_ref[k, :, :length] = high
        rows_ref[k, :, length:] = low.astype(BF16)


def make_tables(filters):
    count, length = filters.shape
    return call(
        table_kernel,
        (count * length * length * 4, count * length * length * 4),
        8,
        out_shape=jax.ShapeDtypeStruct((count, length, 2 * length), BF16),
    )(filters)


def back_kernel(cin_count, *refs):
    pieces = refs[:cin_count]
    rows_ref, matrix_ref, out, grads, parts, parts8, total, bounds, matrix8 = refs[cin_count:]
    step = pl.program_id(0)
    _, length, _ = rows_ref.shape
    out_width = matrix_ref.shape[1]
    seqs = grads.shape[1] // out_width
    tokens = seqs * length

    @pl.when(step == 0)
    def _():
        total[...] = jnp.zeros_like(total)
        block = pieces[0].shape[0]
        for b in range(seqs):
            for r, piece in enumerate(pieces):
                turned = piece[:, b * length : (b + 1) * length].astype(F32).T.astype(BF16)
                columns = spot("cin", r, block, cin_count, b * out_width)
                grads[:length, columns] = turned
                grads[length:, columns] = turned
        gmax = functools.reduce(jnp.maximum, [largest(piece[...]) for piece in pieces])
        bounds[...] = jnp.broadcast_to(gmax, bounds.shape)

    table = rows_ref[pl.ds(GROUP * step, GROUP)]
    reach = functools.reduce(jnp.maximum, reach_of(table, bounds[0:1, 0:1]))
    table = table.reshape(GROUP * length, 2 * length)
    for b in range(seqs):
        high, low = split(dot(table, grads[:, b * out_width : (b + 1) * out_width]))
        low = (low * (65536.0 / reach)).astype(F8)
        for k in range(GROUP):
            source, columns = slice(k * length, (k + 1) * length), slice(k * out_width, (k + 1) * out_width)
            parts[b * length : (b + 1) * length, columns] = high[source]
            parts8[b * length : (b + 1) * length, columns] = low[source]
        if b == 0:
            peak = jnp.max(jnp.abs(matrix_ref[...]).reshape(-1, 16, matrix_ref.shape[2]), axis=0)
            matrix_scale = (256.0 / jnp.maximum(largest(peak), TINY)).astype(BF16)
    back = (reach / 65536.0) / matrix_scale.astype(F32)
    products = []
    for first in range(0, GROUP, 2):
        columns = slice(first * out_width, (first + 2) * out_width)
        products.append(dot(parts[:, columns], matrix_ref[first : first + 2].reshape(2 * out_width, -1)))
        for k in range(first, first + 2):
            matrix8[k * out_width : (k + 1) * out_width] = (matrix_ref[k] * matrix_scale).astype(F8)
    total[...] += functools.reduce(jnp.add, products) + dot(parts8[...], matrix8[...]) * back

    @pl.when(step == pl.num_programs(0) - 1)
    def _():
        summed = total[...]
        exponent = jnp.floor(jnp.log2(jnp.maximum(largest(summed), TINY))) + 1.0
        summed = summed * jnp.exp2(14.0 - exponent)
        if out.shape[1] == tokens + 8:
            block = out.shape[2]
            for j in range(out.shape[0]):
                out[j, :tokens] = summed[:, j * block : (j + 1) * block]
                out[j, tokens:] = jnp.broadcast_to(exponent, (8, block))
        else:
            block = out.shape[1] - 8
            turned = summed.T
            for j in range(out.shape[0]):
                out[j, :block] = turned[j * block : (j + 1) * block]
                out[j, block:] = jnp.broadcast_to(exponent, (8, tokens))


def back_sums(pieces, rows, matrices, cout):
    count, out_width, in_width = matrices.shape
    length = rows.shape[1]
    tokens = pieces[0].shape[1]
    seqs = tokens // length
    own = in_width // cout
    shape = (tokens + 8, own) if own % 128 == 0 else (own + 8, tokens)
    out = jax.ShapeDtypeStruct((cout, *shape), F32)
    return call(
        functools.partial(back_kernel, len(pieces)),
        (4 * count * out_width * in_width * tokens, 2 * matrices.size),
        40,
        out_shape=out,
        grid=(count // GROUP,),
        in_specs=[whole(piece) for piece in pieces]
        + [whole(rows), pl.BlockSpec((GROUP, out_width, in_width), lambda i: (i, 0, 0))],
        out_specs=whole(out),
        scratch_shapes=[
            pltpu.VMEM((2 * length, seqs * out_width), BF16),
            pltpu.VMEM((tokens, GROUP * out_width), BF16),
            pltpu.VMEM((tokens, GROUP * out_width), F8),
            pltpu.VMEM((tokens, in_width), F32),
            pltpu.VMEM((8, length), F32),
            pltpu.VMEM((GROUP * out_width, in_width), F8),
        ],
    )(*pieces, rows, matrices)


def matrix_kernel(cin_count, input_count, cout_count, *refs):
    pieces = refs[:cin_count]
    input_pieces = refs[cin_count : cin_count + input_count]
    rows_ref, out_ref, grads, inputs, inputs8, parts, parts8, bounds = refs[cin_count + input_count :]
    step = pl.program_id(0)
    _, length, _ = rows_ref.shape
    tokens = inputs.shape[0]
    seqs = tokens // length
    out_width = out_ref.shape[1]

    def table_of(first):
        table = rows_ref[pl.ds(first, 2)]
        return table.reshape(2 * length, 2 * length), reach_of(table, bounds[0:1, 0:1])

    def filter_sequence(slot, table, reach, b):
        filtered = lax.dot_general(
            grads[b * out_width : (b + 1) * out_width], table, (((1,), (1,)), ((), ())), preferred_element_type=F32
        )
        high, low = split(filtered)
        place = slice(b * length, (b + 1) * length)
        for k in range(2):
            columns = slice(k * length, (k + 1) * length)
            parts[2 * slot + k, :, place] = high[:, columns]
            parts8[2 * slot + k, :, place] = (low[:, columns] * (65536.0 / reach[k])).astype(F8)

    def filters_of(slot, table, reach):
        return [functools.partial(filter_sequence, slot, table, reach, b) for b in range(seqs)]

    def product(k, back, columns):
        total = dot(parts[k], inputs[:, columns]) + dot(parts8[k], inputs8[:, columns]) * back
        out_ref[k, :, columns] = total.astype(BF16)

    def products_of(slot, reach):
        backs = [(reach[k] / 65536.0) * (bounds[1:2, 0:1] / 256.0) for k in range(2)]
        return [
            functools.partial(product, 2 * slot + k, backs[k], columns)
            for k in range(2)
            for columns in chunks(inputs.shape[1])
        ]

    @pl.when(step == 0)
    def _():
        block = pieces[0].shape[0]
        for r, piece in enumerate(pieces):
            for b in range(seqs):
                rows = spot("cin", r, block, cin_count, b * out_width)
                part = piece[:, b * length : (b + 1) * length]
                grads[rows, :length] = part
                grads[rows, length:] = part
        gmax = functools.reduce(jnp.maximum, [largest(piece[...]) for piece in pieces])
        xmax = functools.reduce(jnp.maximum, [largest(piece[half]) for piece in input_pieces for half in range(piece.shape[0])])
        xmax = jnp.maximum(xmax, TINY)
        bounds[0:1, :] = jnp.broadcast_to(gmax, (1, length))
        bounds[1:2, :] = jnp.broadcast_to(xmax, (1, length))
        block = input_pieces[0].shape[1]
        for r, piece in enumerate(input_pieces):
            for half in range(piece.shape[0]):
                columns = spot("cout", 2 * r + half, block, cout_count)
                turned = piece[half].astype(F32).T
                inputs[:, columns] = turned.astype(BF16)
                inputs8[:, columns] = (turned * (256.0 / xmax)).astype(F8)
        interleave(filters_of(0, *table_of(0)), [])

    now = table_of(GROUP * step)
    late = table_of(GROUP * step + 2)
    coming = table_of(lax.rem(GROUP * step + GROUP, rows_ref.shape[0]))
    interleave(products_of(0, now[1]), filters_of(1, *late))
    interleave(products_of(1, late[1]), filters_of(0, *coming))


def matrix_sums(pieces, input_pieces, rows, cout_count, shape):
    count, out_width, in_width = shape
    length = rows.shape[1]
    tokens = pieces[0].shape[1]
    seqs = tokens // length
    return call(
        functools.partial(matrix_kernel, len(pieces), len(input_pieces), cout_count),
        (3 * count * out_width * in_width * tokens, 2 * count * out_width * in_width),
        32,
        out_shape=jax.ShapeDtypeStruct(shape, BF16),
        grid=(count // GROUP,),
        in_specs=[whole(piece) for piece in (*pieces, *input_pieces)] + [whole(rows)],
        out_specs=pl.BlockSpec((GROUP, out_width, in_width), lambda i: (i, 0, 0)),
        scratch_shapes=[
            pltpu.VMEM((seqs * out_width, 2 * length), BF16),
            pltpu.VMEM((tokens, in_width), BF16),
            pltpu.VMEM((tokens, in_width), F8),
            pltpu.VMEM((GROUP, out_width, tokens), BF16),
            pltpu.VMEM((GROUP, out_width, tokens), F8),
            pltpu.VMEM((8, length), F32),
        ],
    )(*pieces, *input_pieces, rows)


def exchange(array, axis, count, flip):
    return lax.ppermute(array, axis, [(i, i ^ flip) for i in range(count)])


def shards(cin, cout, inputs, cotangent, matrices, filters):
    own, seq_count, length = inputs.shape
    tokens = seq_count * length
    flat_grads = cotangent.reshape(-1, tokens)
    if cin & (cin - 1) or flat_grads.shape[0] % 128:
        pieces = [lax.all_gather(flat_grads, "cin", axis=0, tiled=True)]
    else:
        pieces = [flat_grads] + [exchange(flat_grads, "cin", cin, flip) for flip in range(1, cin)]
    rows = make_tables(lax.optimization_barrier((filters, flat_grads))[0])
    flat_inputs = inputs.reshape(-1, tokens)
    if cout < 2 or cout & (cout - 1) or own % 128:
        input_pieces = [lax.all_gather(flat_inputs, "cout", axis=0, tiled=True)[None]]
        cout_count = 1
    else:
        both = jnp.concatenate([flat_inputs, exchange(flat_inputs, "cout", cout, 1)]).reshape(2, own, tokens)
        input_pieces = [both] + [exchange(both, "cout", cout, flip) for flip in range(2, cout, 2)]
        cout_count = cout

    blocks = back_sums(pieces, rows, matrices, cout).astype(F16)
    came = lax.all_to_all(blocks, "cout", 0, 0, tiled=True)
    matrix_grads = matrix_sums(pieces, input_pieces, rows, cout_count, matrices.shape)
    rows = came.shape[1] - 8
    scales = jnp.exp2(came[:, rows : rows + 1].astype(F32) - 14.0)
    input_grads = jnp.sum(came[:, :rows].astype(F32) * scales, axis=0).astype(BF16)
    if rows == tokens:
        input_grads = input_grads.reshape(seq_count, length, own).transpose(2, 0, 1)
    return (matrix_grads, input_grads.reshape(own, seq_count, length))


def solution(mesh):
    placed = (
        P(("cin", "cout"), None, None),
        P(("cout", "cin"), None, None),
        P(None, "cout", "cin"),
        P(),
    )
    return jax.shard_map(
        functools.partial(shards, mesh.shape["cin"], mesh.shape["cout"]),
        mesh=mesh,
        in_specs=placed,
        out_specs=(P(None, "cout", "cin"), P(("cin", "cout"), None, None)),
        check_vma=False,
    )
```

```python
import functools
import itertools

import jax
import jax.numpy as jnp
from jax import lax
from jax.experimental import pallas as pl
from jax.experimental.pallas import tpu as pltpu
from jax.sharding import PartitionSpec as P

BF16 = jnp.bfloat16
F16 = jnp.float16
F32 = jnp.float32
F8 = jnp.float8_e4m3fn
MIB = 1024 * 1024
GROUP = 4
CHUNK = 512
TINY = 1e-30


def split(wide):
    high = wide.astype(BF16)
    return high, wide - high.astype(F32)


def dot(left, right):
    return jnp.dot(left, right, preferred_element_type=F32)


def call(body, cost, limit, **kwargs):
    flops, moved = cost
    return pl.pallas_call(
        body,
        compiler_params=pltpu.CompilerParams(vmem_limit_bytes=limit * MIB),
        cost_estimate=pl.CostEstimate(flops=flops, bytes_accessed=moved, transcendentals=0),
        **kwargs,
    )


def whole(array):
    return pl.BlockSpec(array.shape, lambda i: (0,) * len(array.shape))


def largest(array):
    return jnp.max(jnp.abs(array.astype(F32)), keepdims=True)


def spot(axis, flip, block, count, base=0):
    if count == 1:
        return slice(base, base + block)
    return pl.ds(pl.multiple_of(base + (lax.axis_index(axis) ^ flip) * block, block), block)


def reach_of(table, gmax):
    length = table.shape[1]
    sums = [jnp.sum(jnp.abs(table[k, 0:1, :length].astype(F32)), keepdims=True) for k in range(table.shape[0])]
    return [jnp.maximum(total * gmax, TINY) for total in sums]


def interleave(first, second):
    for one, other in itertools.zip_longest(first, second):
        for work in (one, other):
            if work is not None:
                work()


def chunks(width):
    size = min(width, CHUNK)
    return [slice(start, start + size) for start in range(0, width, size)]


def table_kernel(filters_ref, rows_ref):
    count, length = filters_ref.shape
    source = lax.broadcasted_iota(jnp.int32, (length, length), 0)
    token = lax.broadcasted_iota(jnp.int32, (length, length), 1)
    for k in range(count):
        spread = jnp.broadcast_to(filters_ref[k : k + 1, :], (length, length))
        shifted = pltpu.roll(spread, 0, 1, stride=1, stride_axis=0)
        high, low = split(jnp.where(token >= source, shifted, 0.0))
        rows_ref[k, :, :length] = high
        rows_ref[k, :, length:] = low.astype(BF16)


def make_tables(filters):
    count, length = filters.shape
    return call(
        table_kernel,
        (count * length * length * 4, count * length * length * 4),
        8,
        out_shape=jax.ShapeDtypeStruct((count, length, 2 * length), BF16),
    )(filters)


def back_kernel(cin_count, *refs):
    pieces = refs[:cin_count]
    rows_ref, matrix_ref, out, grads, parts, parts8, total, bounds, matrix8 = refs[cin_count:]
    step = pl.program_id(0)
    _, length, _ = rows_ref.shape
    out_width = matrix_ref.shape[1]
    seqs = grads.shape[1] // out_width
    tokens = seqs * length

    @pl.when(step == 0)
    def _():
        total[...] = jnp.zeros_like(total)
        block = pieces[0].shape[0]
        for b in range(seqs):
            for r, piece in enumerate(pieces):
                turned = piece[:, b * length : (b + 1) * length].astype(F32).T.astype(BF16)
                columns = spot("cin", r, block, cin_count, b * out_width)
                grads[:length, columns] = turned
                grads[length:, columns] = turned
        gmax = functools.reduce(jnp.maximum, [largest(piece[...]) for piece in pieces])
        bounds[...] = jnp.broadcast_to(gmax, bounds.shape)

    table = rows_ref[pl.ds(GROUP * step, GROUP)]
    reach = functools.reduce(jnp.maximum, reach_of(table, bounds[0:1, 0:1]))
    table = table.reshape(GROUP * length, 2 * length)
    for b in range(seqs):
        high, low = split(dot(table, grads[:, b * out_width : (b + 1) * out_width]))
        low = (low * (65536.0 / reach)).astype(F8)
        for k in range(GROUP):
            source, columns = slice(k * length, (k + 1) * length), slice(k * out_width, (k + 1) * out_width)
            parts[b * length : (b + 1) * length, columns] = high[source]
            parts8[b * length : (b + 1) * length, columns] = low[source]
        if b == 0:
            peak = jnp.max(jnp.abs(matrix_ref[...]).reshape(-1, 16, matrix_ref.shape[2]), axis=0)
            matrix_scale = (256.0 / jnp.maximum(largest(peak), TINY)).astype(BF16)
    back = (reach / 65536.0) / matrix_scale.astype(F32)
    products = []
    for first in range(0, GROUP, 2):
        columns = slice(first * out_width, (first + 2) * out_width)
        products.append(dot(parts[:, columns], matrix_ref[first : first + 2].reshape(2 * out_width, -1)))
        for k in range(first, first + 2):
            matrix8[k * out_width : (k + 1) * out_width] = (matrix_ref[k] * matrix_scale).astype(F8)
    total[...] += functools.reduce(jnp.add, products) + dot(parts8[...], matrix8[...]) * back

    @pl.when(step == pl.num_programs(0) - 1)
    def _():
        summed = total[...]
        exponent = jnp.floor(jnp.log2(jnp.maximum(largest(summed), TINY))) + 1.0
        summed = summed * jnp.exp2(14.0 - exponent)
        if out.shape[1] == tokens + 8:
            block = out.shape[2]
            for j in range(out.shape[0]):
                out[j, :tokens] = summed[:, j * block : (j + 1) * block]
                out[j, tokens:] = jnp.broadcast_to(exponent, (8, block))
        else:
            block = out.shape[1] - 8
            turned = summed.T
            for j in range(out.shape[0]):
                out[j, :block] = turned[j * block : (j + 1) * block]
                out[j, block:] = jnp.broadcast_to(exponent, (8, tokens))


def back_sums(pieces, rows, matrices, cout):
    count, out_width, in_width = matrices.shape
    length = rows.shape[1]
    tokens = pieces[0].shape[1]
    seqs = tokens // length
    own = in_width // cout
    shape = (tokens + 8, own) if own % 128 == 0 else (own + 8, tokens)
    out = jax.ShapeDtypeStruct((cout, *shape), F32)
    return call(
        functools.partial(back_kernel, len(pieces)),
        (4 * count * out_width * in_width * tokens, 2 * matrices.size),
        40,
        out_shape=out,
        grid=(count // GROUP,),
        in_specs=[whole(piece) for piece in pieces]
        + [whole(rows), pl.BlockSpec((GROUP, out_width, in_width), lambda i: (i, 0, 0))],
        out_specs=whole(out),
        scratch_shapes=[
            pltpu.VMEM((2 * length, seqs * out_width), BF16),
            pltpu.VMEM((tokens, GROUP * out_width), BF16),
            pltpu.VMEM((tokens, GROUP * out_width), F8),
            pltpu.VMEM((tokens, in_width), F32),
            pltpu.VMEM((8, length), F32),
            pltpu.VMEM((GROUP * out_width, in_width), F8),
        ],
    )(*pieces, rows, matrices)


def matrix_kernel(cin_count, input_count, cout_count, *refs):
    pieces = refs[:cin_count]
    input_pieces = refs[cin_count : cin_count + input_count]
    rows_ref, out_ref, grads, inputs, inputs8, parts, parts8, bounds = refs[cin_count + input_count :]
    step = pl.program_id(0)
    _, length, _ = rows_ref.shape
    tokens = inputs.shape[0]
    seqs = tokens // length
    out_width = out_ref.shape[1]

    def table_of(first):
        table = rows_ref[pl.ds(first, 2)]
        return table.reshape(2 * length, 2 * length), reach_of(table, bounds[0:1, 0:1])

    def filter_sequence(slot, table, reach, b):
        filtered = lax.dot_general(
            grads[b * out_width : (b + 1) * out_width], table, (((1,), (1,)), ((), ())), preferred_element_type=F32
        )
        high, low = split(filtered)
        place = slice(b * length, (b + 1) * length)
        for k in range(2):
            columns = slice(k * length, (k + 1) * length)
            parts[2 * slot + k, :, place] = high[:, columns]
            parts8[2 * slot + k, :, place] = (low[:, columns] * (65536.0 / reach[k])).astype(F8)

    def filters_of(slot, table, reach):
        return [functools.partial(filter_sequence, slot, table, reach, b) for b in range(seqs)]

    def product(k, back, columns):
        total = dot(parts[k], inputs[:, columns]) + dot(parts8[k], inputs8[:, columns]) * back
        out_ref[k, :, columns] = total.astype(BF16)

    def products_of(slot, reach):
        backs = [(reach[k] / 65536.0) * (bounds[1:2, 0:1] / 256.0) for k in range(2)]
        return [
            functools.partial(product, 2 * slot + k, backs[k], columns)
            for k in range(2)
            for columns in chunks(inputs.shape[1])
        ]

    @pl.when(step == 0)
    def _():
        block = pieces[0].shape[0]
        for r, piece in enumerate(pieces):
            for b in range(seqs):
                rows = spot("cin", r, block, cin_count, b * out_width)
                part = piece[:, b * length : (b + 1) * length]
                grads[rows, :length] = part
                grads[rows, length:] = part
        gmax = functools.reduce(jnp.maximum, [largest(piece[...]) for piece in pieces])
        xmax = functools.reduce(jnp.maximum, [largest(piece[half]) for piece in input_pieces for half in range(piece.shape[0])])
        xmax = jnp.maximum(xmax, TINY)
        bounds[0:1, :] = jnp.broadcast_to(gmax, (1, length))
        bounds[1:2, :] = jnp.broadcast_to(xmax, (1, length))
        block = input_pieces[0].shape[1]
        for r, piece in enumerate(input_pieces):
            for half in range(piece.shape[0]):
                columns = spot("cout", 2 * r + half, block, cout_count)
                turned = piece[half].astype(F32).T
                inputs[:, columns] = turned.astype(BF16)
                inputs8[:, columns] = (turned * (256.0 / xmax)).astype(F8)
        interleave(filters_of(0, *table_of(0)), [])

    now = table_of(GROUP * step)
    late = table_of(GROUP * step + 2)
    coming = table_of(lax.rem(GROUP * step + GROUP, rows_ref.shape[0]))
    interleave(products_of(0, now[1]), filters_of(1, *late))
    interleave(products_of(1, late[1]), filters_of(0, *coming))


def matrix_sums(pieces, input_pieces, rows, cout_count, shape):
    count, out_width, in_width = shape
    length = rows.shape[1]
    tokens = pieces[0].shape[1]
    seqs = tokens // length
    return call(
        functools.partial(matrix_kernel, len(pieces), len(input_pieces), cout_count),
        (3 * count * out_width * in_width * tokens, 2 * count * out_width * in_width),
        32,
        out_shape=jax.ShapeDtypeStruct(shape, BF16),
        grid=(count // GROUP,),
        in_specs=[whole(piece) for piece in (*pieces, *input_pieces)] + [whole(rows)],
        out_specs=pl.BlockSpec((GROUP, out_width, in_width), lambda i: (i, 0, 0)),
        scratch_shapes=[
            pltpu.VMEM((seqs * out_width, 2 * length), BF16),
            pltpu.VMEM((tokens, in_width), BF16),
            pltpu.VMEM((tokens, in_width), F8),
            pltpu.VMEM((GROUP, out_width, tokens), BF16),
            pltpu.VMEM((GROUP, out_width, tokens), F8),
            pltpu.VMEM((8, length), F32),
        ],
    )(*pieces, *input_pieces, rows)


def exchange(array, axis, count, flip):
    return lax.ppermute(array, axis, [(i, i ^ flip) for i in range(count)])


def shards(cin, cout, inputs, cotangent, matrices, filters):
    own, seq_count, length = inputs.shape
    tokens = seq_count * length
    flat_grads = cotangent.reshape(-1, tokens)
    if cin & (cin - 1) or flat_grads.shape[0] % 128:
        pieces = [lax.all_gather(flat_grads, "cin", axis=0, tiled=True)]
    else:
        pieces = [flat_grads] + [exchange(flat_grads, "cin", cin, flip) for flip in range(1, cin)]
    rows = make_tables(lax.optimization_barrier((filters, flat_grads))[0])
    flat_inputs = inputs.reshape(-1, tokens)
    if cout < 2 or cout & (cout - 1) or own % 128:
        input_pieces = [lax.all_gather(flat_inputs, "cout", axis=0, tiled=True)[None]]
        cout_count = 1
    else:
        both = jnp.concatenate([flat_inputs, exchange(flat_inputs, "cout", cout, 1)]).reshape(2, own, tokens)
        input_pieces = [both] + [exchange(both, "cout", cout, flip) for flip in range(2, cout, 2)]
        cout_count = cout

    blocks = back_sums(pieces, rows, matrices, cout).astype(F16)
    came = lax.all_to_all(blocks, "cout", 0, 0, tiled=True)
    matrix_grads = matrix_sums(pieces, input_pieces, rows, cout_count, matrices.shape)
    rows = came.shape[1] - 8
    scales = jnp.exp2(came[:, rows : rows + 1].astype(F32) - 14.0)
    input_grads = jnp.sum(came[:, :rows].astype(F32) * scales, axis=0).astype(BF16)
    if rows == tokens:
        input_grads = input_grads.reshape(seq_count, length, own).transpose(2, 0, 1)
    return (matrix_grads, input_grads.reshape(own, seq_count, length))


def solution(mesh):
    placed = (
        P(("cin", "cout"), None, None),
        P(("cout", "cin"), None, None),
        P(None, "cout", "cin"),
        P(),
    )
    return jax.shard_map(
        functools.partial(shards, mesh.shape["cin"], mesh.shape["cout"]),
        mesh=mesh,
        in_specs=placed,
        out_specs=(P(None, "cout", "cin"), P(("cin", "cout"), None, None)),
        check_vma=False,
    )
```
